32 devices in a mesh: band: 4 (over x, core), dx: 2 (over y), dyz: 4 (over z).
Axes of the slice: x: 2, y: 2, z: 4, core: 2. Of those that a mesh axis runs over, the one named last changes fastest.
Arguments:
- density: float32 [64, 96, 512], P('dx', 'dyz', 'band'), may hold values from 0.1 to 3
- hartree: float32 [64, 96, 512], P('dx', 'dyz', 'band'), may hold values from -6 to 6
- box_root: int32 [3, 512], P(None, ('dx', 'dyz')), may hold values from 0 to 511, as said below
- species: int32 [512], P(('dx', 'dyz')), may hold values from 0 to 1
- atom_count: int32 [8], P(('dx', 'dyz')), may hold values from 1 to 64, 256 in all
- shape_functions: float32 [2, 25, 4096], replicated, may hold values from -28 to 28
- coupling: float32 [2, 25, 256], replicated, may hold values from -1.25 to 1.25
- coulomb: float32 [2, 256, 256], replicated, may hold values from -0.375 to 0.375
- rho_ij: float32 [512, 256], P(('dx', 'dyz')), may hold values from -6 to 6
- projections: float32 [512, 16, 512], P(('dx', 'dyz'), None, 'band'), may hold values from -6 to 6
Outputs:
- potential: float32 [64, 96, 512], P('dx', 'dyz', 'band')
- atom_hamiltonian: float32 [512, 256], P(('dx', 'dyz'))
- applied: float32 [512, 16, 512], P(('dx', 'dyz'), None, 'band')
The draws below stay inside these ranges and needn't reach their ends.
Inputs may be any that keep to these rules, and one draw needn't show every extreme that they name: Atom a's first two box_root entries lie within the first- and second-dimension cells held by the devices that hold atom a; the third is any cell of the third dimension. Domain column c holds its atoms in slots c * 64 to c * 64 + atom_count[c] - 1; its other slots are empty.
All inputs are finite; a program needn't handle non-finite values. No bound on the sum of `atom_count` on one device may be relied on, other than what follows from the above.
Results may differ from the reference program's by a relative error of at most 0.0003.
Values sent between devices are 32-bit elements; how exact they have to be, the bound alone decides.
A program may use at most 64 MiB of HBM per device.

```python
import math
import jax
import jax.numpy as jnp
import numpy as np
from jax import lax

CX = 32
CY = 24
BOX = 16
NL = 25
NI = 16
NSPEC = 2
ATOM_DEV = 64
NX = 64
NY = 96
NZ = 512
COLUMNS = 8
ATOMS = 512
BANDS = 512
N_DYZ = 4


def draw_box_root(key, part):
    key = jax.random.fold_in(key, 11)
    slots = jnp.arange(ATOMS, dtype=jnp.int32)
    column = slots // ATOM_DEV
    start_x = column // N_DYZ * CX
    start_y = column % N_DYZ * CY
    keys = jax.random.split(key, 3)
    offset_x = jax.random.randint(keys[0], (ATOMS,), 0, CX, dtype=jnp.int32)
    offset_y = jax.random.randint(keys[1], (ATOMS,), 0, CY, dtype=jnp.int32)
    offset_z = jax.random.randint(keys[2], (ATOMS,), 0, NZ, dtype=jnp.int32)
    offset_x = offset_x.at[0].set(0).at[ATOMS - 1].set(CX - 1)
    offset_y = offset_y.at[0].set(0).at[ATOMS - 1].set(CY - 1)
    offset_z = offset_z.at[0].set(0).at[ATOMS - 1].set(NZ - 1)
    return jnp.stack([start_x + offset_x, start_y + offset_y, offset_z]).astype(jnp.int32)


def set_ends(values, stream_key, smallest, high):
    index_at = [jax.random.randint(jax.random.fold_in(stream_key, axis), (), 0, length) for axis, length in enumerate(values.shape)]
    main_axis = values.shape.index(max(values.shape))
    beside = index_at[:main_axis] + [(index_at[main_axis] + 1) % values.shape[main_axis]] + index_at[main_axis + 1:]
    return values.at[tuple(index_at)].set(smallest).at[tuple(beside)].set(high)


def level_of(own_key, shape, cuts, smallest, top_value):
    factor_of = 1.0
    for dim, blocks in cuts:
        steps = jax.random.uniform(jax.random.fold_in(jax.random.fold_in(own_key, 6), dim), (blocks,), jnp.float32, smallest / len(cuts), top_value / len(cuts))
        factor_of = factor_of * jnp.repeat(jnp.exp(steps), shape[dim] // blocks).reshape((-1,) + (1,) * (len(shape) - 1 - dim))
    return factor_of


def profile(number_of, total, most, lean):
    loads = [(1 << 20) // math.isqrt(rank ** lean) + 1 for rank in range(2, number_of + 1)]
    spare, given = total - most - (number_of - 1), [1] * (number_of - 1)
    while spare > 0:
        free = [i for i in range(number_of - 1) if given[i] < most]
        pool, remaining = sum([loads[i] for i in free]), spare
        for i in free:
            addition = min(most - given[i], max(1, remaining * loads[i] // pool), spare)
            given[i] = given[i] + addition
            spare = spare - addition
    return np.array([most] + given)


def uneven_parts(rng, number_of, total, most, lean):
    if number_of == 2:
        one = jax.random.randint(rng, (), max(1, total - most), min(most, total - 1) + 1)
        return jnp.stack([one, total - one])
    lengths = jnp.asarray(profile(number_of, total, most, lean), jnp.int32)
    twos = (number_of - 1) // 2
    donor, sink = lengths[1:1 + 2 * twos:2], lengths[2:2 + 2 * twos:2]
    margin = jnp.minimum(donor - 1, most - sink)
    passed = jax.random.randint(jax.random.fold_in(rng, 1), (twos,), 0, 1 << 20) % (margin + 1)
    lengths = lengths.at[1:1 + 2 * twos:2].set(donor - passed).at[2:2 + 2 * twos:2].set(sink + passed)
    return lengths[jax.random.permutation(jax.random.fold_in(rng, 2), number_of)]


def gaussian(stream_key, extent, width, most, pieces=(), held_as=jnp.bfloat16):
    array = width * jax.random.normal(stream_key, extent, jnp.float32)
    if pieces:
        array = array * level_of(stream_key, extent, pieces, -0.22, 0.18)
    return jnp.clip(array, -most, most).astype(held_as)


def setup_inputs(seed: int = 0) -> dict:
    splits = jax.random.split(jax.random.key(seed), 11)
    return {
        "density": jnp.clip(jnp.exp(math.log(3.0) - 3.4011974 * jax.random.uniform(splits[0], (NX, NY, NZ), jnp.float32) ** level_of(splits[0], (NX, NY, NZ), ((0, 2), (1, 4), (2, 4)), -0.2, 0.2)), 0.1, 3.0),
        "hartree": gaussian(splits[1], (NX, NY, NZ), 1.0, 6.0, ((0, 2), (1, 4), (2, 4)), jnp.float32),
        "box_root": draw_box_root(jax.random.fold_in(splits[10], 71), 0),
        "species": set_ends(jax.random.randint(splits[3], (ATOMS,), 0, NSPEC), jax.random.fold_in(splits[3], 1), 0, NSPEC - 1).astype(jnp.int32),
        "atom_count": uneven_parts(splits[4], COLUMNS, COLUMNS * ATOM_DEV // 2, ATOM_DEV, 2).astype(jnp.int32),
        "shape_functions": gaussian(splits[5], (NSPEC, NL, BOX * BOX * BOX), (296.0 / BOX ** 1.5), 28.0, (), jnp.float32),
        "coupling": gaussian(splits[6], (NSPEC, NL, NI * NI), NL ** -0.5, 1.25, (), jnp.float32),
        "coulomb": gaussian(splits[7], (NSPEC, NI * NI, NI * NI), (NI * NI) ** -0.5, 0.375, (), jnp.float32),
        "rho_ij": gaussian(splits[8], (ATOMS, NI * NI), 1.0, 6.0, ((0, 8),), jnp.float32),
        "projections": gaussian(splits[9], (ATOMS, NI, BANDS), 1.0, 6.0, ((0, 8), (2, 4)), jnp.float32),
    }


GRID_H = 0.15
KAPPA = 0.804
MU_COEF = 0.2195149727645171
PRECISE = lax.Precision.HIGHEST

def exchange_energy(dens, sigma):
    prefactor = -0.75 * (3.0 / jnp.pi) ** (1.0 / 3.0)
    reduced = sigma / (4.0 * (3.0 * jnp.pi ** 2) ** (2.0 / 3.0) * dens ** (8.0 / 3.0))
    enhance = 1.0 + KAPPA - KAPPA / (1.0 + MU_COEF * reduced / KAPPA)
    return prefactor * dens ** (4.0 / 3.0) * enhance

def energy_slopes(dens, sigma):

    def summed(dens_in, sigma_in):
        return jnp.sum(exchange_energy(dens_in, sigma_in))
    return jax.grad(summed, argnums=(0, 1))(dens, sigma)

def hamiltonian_blocks(moments, rho_rows, picks, live, coupling, coulomb):
    summed = jnp.zeros((moments.shape[0], coulomb.shape[2]), moments.dtype)
    for spec_id in range(coupling.shape[0]):
        term = jnp.dot(moments, coupling[spec_id], precision=PRECISE) + 2.0 * jnp.dot(rho_rows, coulomb[spec_id], precision=PRECISE)
        summed = summed + picks[:, spec_id:spec_id + 1] * term
    return jnp.where(live[:, None], summed, 0.0)

def reference(density, hartree, box_root, species, atom_count, shape_functions, coupling, coulomb, rho_ij, projections):
    half_step = 0.5 / GRID_H
    grads = [(jnp.roll(density, -1, axis_dim) - jnp.roll(density, 1, axis_dim)) * half_step for axis_dim in range(3)]
    sigma = grads[0] * grads[0] + grads[1] * grads[1] + grads[2] * grads[2]
    slope_n, slope_s = energy_slopes(density, sigma)
    spread = jnp.zeros_like(density)
    for axis_dim in range(3):
        flux = slope_s * grads[axis_dim]
        spread = spread + (jnp.roll(flux, -1, axis_dim) - jnp.roll(flux, 1, axis_dim)) * half_step
    potential = hartree + slope_n - 2.0 * spread
    flat_shapes = shape_functions.reshape(NSPEC * NL, BOX * BOX * BOX)
    box_steps = jnp.arange(BOX, dtype=jnp.int32)
    spec_ids = jnp.arange(NSPEC, dtype=jnp.int32)

    def one_atom(inputs):
        root, species_id = inputs
        index_x = ((root[0] + box_steps) % NX).astype(jnp.int32)
        index_y = ((root[1] + box_steps) % NY).astype(jnp.int32)
        index_z = ((root[2] + box_steps) % NZ).astype(jnp.int32)
        window = potential[index_x][:, index_y][:, :, index_z].reshape(BOX * BOX * BOX)
        every = jnp.dot(flat_shapes, window, precision=PRECISE).reshape(NSPEC, NL)
        picks = (spec_ids == species_id).astype(every.dtype)
        return lax.optimization_barrier(jnp.sum(every * picks[:, None], axis=0)) * GRID_H ** 3
    moments = lax.map(one_atom, (box_root.T, species))
    slots = jnp.arange(ATOMS, dtype=jnp.int32)
    column = (slots // ATOM_DEV).astype(jnp.int32)
    live = slots % ATOM_DEV < atom_count[column]
    picks = (species[:, None] == spec_ids[None, :]).astype(moments.dtype)
    atom_hamiltonian = hamiltonian_blocks(moments, rho_ij, picks, live, coupling, coulomb)
    blocks = atom_hamiltonian.reshape(ATOMS, NI, NI)
    applied = jnp.einsum('aij,ajn->ain', blocks, projections, precision=PRECISE)
    return (potential, atom_hamiltonian, applied)
```

```python
import functools
import math

import jax
import jax.numpy as jnp
from jax import lax
from jax.experimental import pallas as pl
from jax.experimental.pallas import tpu as pltpu
from jax.sharding import PartitionSpec as P

BOX = 16
NI = 16
GROUP = 16
PAD = 16
GRID_H = 0.15
KAPPA = 0.804
MU_COEF = 0.2195149727645171
PRECISE = lax.Precision.HIGHEST
HALF = 0.5 / GRID_H
PREF = -0.75 * (3.0 / math.pi) ** (1.0 / 3.0)
RED = 4.0 * (3.0 * math.pi**2) ** (2.0 / 3.0)
MESH = pl.DeviceIdType.MESH
VMEM_LIMIT = 48 * 1024 * 1024


def iota(shape, dim):
    return lax.broadcasted_iota(jnp.int32, shape, dim)


def shifted(axis, step):
    size = lax.axis_size(axis)
    return lax.rem(lax.axis_index(axis) + (step + size), size)


def enter(devices):
    barrier = pltpu.get_barrier_semaphore()
    for device in devices:
        pl.semaphore_signal(barrier, inc=1, device_id=device, device_id_type=MESH)
    pl.semaphore_wait(barrier, len(devices))


def split(value):
    high = value.astype(jnp.bfloat16)
    return high, (value - high.astype(jnp.float32)).astype(jnp.bfloat16)


def mm(a, b):
    return jnp.dot(a, b, preferred_element_type=jnp.float32)


def pack_ends(ref):
    wx, wy, depth = ref.shape
    lane = iota((wy, depth), 1)
    packed = jnp.zeros((wy, depth), jnp.float32)
    for x in range(wx):
        moved = pltpu.roll(ref[x], 2 * x + 1, 1)
        packed = jnp.where((lane == 2 * x) | (lane == 2 * x + 1), moved, packed)
    return packed


def join_ends(before, after):
    lane = iota(before.shape, 1)
    depth = before.shape[1]
    return jnp.where(
        lax.rem(lane, 2) == 1, pltpu.roll(before, 1, 1), pltpu.roll(after, depth - 1, 1)
    )


def grid_kernel(
    dens_ref, hart_ref, root_ref, species_ref, count_ref,
    pot_ref, list_ref,
    dpad, fxp, fyp, fz, slope_n_ref,
    send_x, send_y, send_z, recv_x, recv_y, recv_z,
    gsend_x, gsend_y, gsend_z, grecv_x, grecv_y, grecv_z,
    plan_send, plan_recv, send_sems, recv_sems,
):
    wx, wy, depth = dens_ref.shape
    up_x, down_x = {"dx": shifted("dx", 1)}, {"dx": shifted("dx", -1)}
    up_y, down_y = {"dyz": shifted("dyz", 1)}, {"dyz": shifted("dyz", -1)}
    up_z, down_z = {"band": shifted("band", 1)}, {"band": shifted("band", -1)}
    up_xy = {"dx": shifted("dx", 1), "dyz": shifted("dyz", 1)}
    down_xy = {"dx": shifted("dx", -1), "dyz": shifted("dyz", -1)}
    slots = root_ref.shape[1]

    def remote(src, dst, sem, device):
        copy = pltpu.make_async_remote_copy(
            src_ref=src, dst_ref=dst, send_sem=send_sems.at[sem], recv_sem=recv_sems.at[sem],
            device_id=device, device_id_type=MESH,
        )
        copy.start()
        return copy

    send_x[0] = dens_ref[wx - 1]
    send_x[1] = dens_ref[0]
    send_y[0] = dens_ref[:, wy - 1, :]
    send_y[1] = dens_ref[:, 0, :]
    send_z[...] = pack_ends(dens_ref)
    plan_send[...] = jnp.zeros_like(plan_send)
    plan_send[0:1, 0:slots] = root_ref[0:1, :] - lax.axis_index("dx") * wx
    plan_send[1:2, 0:slots] = root_ref[1:2, :] - lax.axis_index("dyz") * wy
    plan_send[2:3, 0:slots] = root_ref[2:3, :]
    plan_send[3:4, 0:slots] = species_ref[...]
    plan_send[4:5, :] = jnp.full((1, 128), count_ref[0], jnp.int32)

    enter([up_x, down_x, up_y, down_y, up_z, down_z, up_xy, down_xy])
    first = [
        remote(send_z, recv_z.at[0], 0, up_z),
        remote(send_z, recv_z.at[1], 1, down_z),
        remote(send_y.at[0], recv_y.at[0], 2, up_y),
        remote(send_y.at[1], recv_y.at[1], 3, down_y),
        remote(send_x.at[0], recv_x.at[0], 4, up_x),
        remote(send_x.at[1], recv_x.at[1], 5, down_x),
    ]
    plans = [
        remote(plan_send, plan_recv.at[0], 6, up_x),
        remote(plan_send, plan_recv.at[1], 7, up_y),
        remote(plan_send, plan_recv.at[2], 8, up_xy),
    ]
    dpad[1 : wx + 1, 8 : wy + 8, :] = dens_ref[...]
    for copy in first:
        copy.wait()
    dpad[0, 8 : wy + 8, :] = recv_x[0]
    dpad[wx + 1, 8 : wy + 8, :] = recv_x[1]
    dpad[1 : wx + 1, 7, :] = recv_y[0]
    dpad[1 : wx + 1, wy + 8, :] = recv_y[1]
    ends = join_ends(recv_z[0], recv_z[1])
    lane = iota((wy, depth), 1)

    def flux_step(x):
        here = dpad[x + 1, 8 : wy + 8, :]
        gx = (dpad[x + 2, 8 : wy + 8, :] - dpad[x, 8 : wy + 8, :]) * HALF
        gy = (dpad[x + 1, 9 : wy + 9, :] - dpad[x + 1, 7 : wy + 7, :]) * HALF
        end = pltpu.roll(ends, depth - 1 - 2 * x, 1)
        after = jnp.where(lane == depth - 1, end, pltpu.roll(here, depth - 1, 1))
        before = jnp.where(lane == 0, end, pltpu.roll(here, 1, 1))
        gz = (after - before) * HALF
        sigma = gx * gx + gy * gy + gz * gz
        log_n = jnp.log(here)
        cube = jnp.exp(log_n * (1.0 / 3.0))
        inv = 1.0 / (here * cube)
        r = sigma * inv * inv * (1.0 / RED)
        u = 1.0 / (1.0 + (MU_COEF / KAPPA) * r)
        slope_r = MU_COEF * u * u
        slope_s = (PREF / RED) * slope_r * inv
        enhance = 1.0 + KAPPA - KAPPA * u
        slope_n_ref[x] = (4.0 / 3.0 * PREF) * cube * (enhance - 2.0 * r * slope_r)
        fxp[x + 1] = slope_s * gx
        fyp[x, 8 : wy + 8, :] = slope_s * gy
        fz[x] = slope_s * gz

    per = 4

    def flux_steps(t, carry):
        for k in range(per):
            flux_step(t * per + k)
        return carry

    lax.fori_loop(0, wx // per, flux_steps, 0)

    gsend_x[0] = fxp[wx]
    gsend_x[1] = fxp[1]
    gsend_y[0] = fyp[:, wy + 7, :]
    gsend_y[1] = fyp[:, 8, :]
    gsend_z[...] = pack_ends(fz)
    second = [
        remote(gsend_z, grecv_z.at[0], 9, up_z),
        remote(gsend_z, grecv_z.at[1], 10, down_z),
        remote(gsend_y.at[0], grecv_y.at[0], 11, up_y),
        remote(gsend_y.at[1], grecv_y.at[1], 12, down_y),
        remote(gsend_x.at[0], grecv_x.at[0], 13, up_x),
        remote(gsend_x.at[1], grecv_x.at[1], 14, down_x),
    ]

    for copy in plans:
        copy.wait()
    depth_all = depth * lax.axis_size("band")
    first_z = lax.axis_index("band") * depth
    columns = []
    for c in range(4):
        plan = plan_send[...] if c == 0 else plan_recv[c - 1]
        x = plan[0:1, :] - (wx if c in (1, 3) else 0)
        y = plan[1:2, :] - (wy if c in (2, 3) else 0)
        z = plan[2:3, :] - first_z
        z = jnp.where(z < 0, z + depth_all, z)
        slot = iota((1, 128), 1)
        meets = (slot < plan[4:5, :]) & (slot < slots)
        meets &= (x > -BOX) & (y > -BOX) & (x < wx) & (y < wy)
        meets &= (z < depth) | (z > depth_all - BOX)
        rows = (x + PAD) * (wy + 2 * PAD) + (y + PAD)
        dest = 8 + c * slots + slot
        columns.append((meets, rows, z, dest, plan[3:4, :]))
    meets, rows, z, dest, kind = [jnp.concatenate([c[f].astype(jnp.int32) for c in columns], 1) for f in range(5)]
    wide = 4 * 128
    upper = (iota((wide, wide), 0) <= iota((wide, wide), 1)).astype(jnp.bfloat16)
    row8 = iota((8, wide), 0)
    picked = jnp.where((meets == 1) & (kind == row8), 1.0, 0.0)
    order = mm(picked.astype(jnp.bfloat16), upper)
    fields = jnp.where(row8 == 0, rows, jnp.where(row8 == 1, z, jnp.where(row8 == 2, dest, 0)))
    fields = fields.astype(jnp.float32)
    for s in range(2):
        total = jnp.sum(picked[s : s + 1, :], axis=1, keepdims=True)
        place = iota((256, wide), 0).astype(jnp.float32) + 1.0
        onehot = jnp.where((order[s : s + 1, :] == place) & (picked[s : s + 1, :] > 0.5), 1.0, 0.0)
        got = lax.dot_general(
            fields, onehot, (((1,), (1,)), ((), ())), precision=PRECISE,
            preferred_element_type=jnp.float32,
        )
        got = jnp.where(iota((8, 256), 0) == 3, total, got)
        list_ref[s] = (got + 0.5).astype(jnp.int32)

    for copy in second:
        copy.wait()
    fxp[0] = grecv_x[0]
    fxp[wx + 1] = grecv_x[1]
    fyp[:, 7, :] = grecv_y[0]
    fyp[:, wy + 8, :] = grecv_y[1]
    flux_ends = join_ends(grecv_z[0], grecv_z[1])

    def pot_step(x):
        here = fz[x]
        end = pltpu.roll(flux_ends, depth - 1 - 2 * x, 1)
        after = jnp.where(lane == depth - 1, end, pltpu.roll(here, depth - 1, 1))
        before = jnp.where(lane == 0, end, pltpu.roll(here, 1, 1))
        spread = (fxp[x + 2] - fxp[x]) * HALF
        spread = spread + (fyp[x, 9 : wy + 9, :] - fyp[x, 7 : wy + 7, :]) * HALF
        spread = spread + (after - before) * HALF
        pot_ref[x] = hart_ref[x] + slope_n_ref[x] - 2.0 * spread

    def pot_steps(t, carry):
        for k in range(per):
            pot_step(t * per + k)
        return carry

    lax.fori_loop(0, wx // per, pot_steps, 0)


def moment_kernel(
    depth_all, list_ref, pot_ref, high_ref, low_ref, out_pot_ref, out_ref, padded, gathered, folded, sums
):
    wx, wy, depth = pot_ref.shape
    rows_y = wy + 2 * PAD
    comps = high_ref.shape[1] // BOX
    out_pot_ref[...] = pot_ref[...]
    padded[...] = jnp.zeros_like(padded)
    for x in range(wx):
        start = (x + PAD) * rows_y + PAD
        padded[start : start + wy, :] = pot_ref[x]
    sums[...] = jnp.zeros_like(sums)
    folded[...] = jnp.zeros_like(folded)
    lanes = GROUP * BOX
    lane = iota((BOX, 128), 1)
    adder = (iota((GROUP, lanes), 0) == iota((GROUP, lanes), 1) // BOX).astype(jnp.float32)
    keep = lax.rem(iota((BOX, lanes), 1), BOX) == iota((BOX, lanes), 0)

    for s in range(2):
        total = list_ref[s, 3, 0]

        def one_group(g, carry, s=s, total=total):
            gathered[...] = jnp.zeros_like(gathered)
            for q in range(GROUP):
                p = g * GROUP + q

                @pl.when(p < total)
                def _(q=q, p=p):
                    row = list_ref[s, 0, p]
                    z = list_ref[s, 1, p]
                    left = (q * BOX) % 128
                    tile = q * BOX // 128 * 128
                    shift = lax.rem(left + depth_all - z, depth)
                    cell = z + lane - left
                    cell = jnp.where(cell >= depth_all, cell - depth_all, cell)
                    mine = (lane >= left) & (lane < left + BOX) & (cell < depth)
                    for i in range(BOX):
                        piece = padded[pl.ds(row + i * rows_y, BOX), :]
                        piece = pltpu.roll(piece, shift, 1)
                        spot = (slice(i * BOX, (i + 1) * BOX), slice(tile, tile + 128))
                        gathered[spot] = jnp.where(mine, piece, gathered[spot])

            g_high, g_low = split(gathered[...])
            product = mm(high_ref[s], g_high) + (mm(high_ref[s], g_low) + mm(low_ref[s], g_high))
            product = jnp.where(keep[None], product.reshape(comps, BOX, lanes), 0.0)
            folded[0:comps, :] = jnp.sum(product, axis=1)
            result = lax.dot_general(
                adder, folded[...], (((1,), (1,)), ((), ())), precision=PRECISE,
                preferred_element_type=jnp.float32,
            ) * (GRID_H**3)
            for q in range(GROUP):
                spot = list_ref[s, 2, g * GROUP + q]
                sums[pl.ds(spot, 1), :] = result[q : q + 1, :]
            return carry

        lax.fori_loop(0, (total + GROUP - 1) // GROUP, one_group, 0)
    slots = out_ref.shape[1]
    for c in range(4):
        out_ref[c] = sums[8 + c * slots : 8 + (c + 1) * slots, :]


def block_kernel(
    part_ref, species_ref, count_ref, coupling_ref, coulomb_ref, rho_ref, ham_ref,
    around, parts, total_ref, cpad, send_sems, recv_sems,
):
    bands = lax.axis_size("band")
    me = lax.axis_index("band")
    slots = part_ref.shape[1]
    up_x, down_x = {"dx": shifted("dx", 1)}, {"dx": shifted("dx", -1)}
    up_y, down_y = {"dyz": shifted("dyz", 1)}, {"dyz": shifted("dyz", -1)}
    up_xy = {"dx": shifted("dx", 1), "dyz": shifted("dyz", 1)}
    down_xy = {"dx": shifted("dx", -1), "dyz": shifted("dyz", -1)}
    others = [{"band": shifted("band", t)} for t in range(1, bands)]
    enter([up_x, down_x, up_y, down_y, up_xy, down_xy] + others)

    def remote(src, dst, sem, device):
        copy = pltpu.make_async_remote_copy(
            src_ref=src, dst_ref=dst, send_sem=send_sems.at[sem], recv_sem=recv_sems.at[sem],
            device_id=device, device_id_type=MESH,
        )
        copy.start()
        return copy

    copies = [
        remote(part_ref.at[c + 1], around.at[c], c, device)
        for c, device in enumerate((down_x, down_y, down_xy))
    ]
    eye = iota((slots, slots), 0) == iota((slots, slots), 1)
    kind = jnp.sum(jnp.where(eye, species_ref[...], 0), axis=1, keepdims=True)
    live = iota((slots, 1), 0) < count_ref[0]
    cpad[...] = jnp.zeros_like(cpad)
    comps = coupling_ref.shape[1]
    rho_high, rho_low = split(rho_ref[...])
    coul = jnp.zeros(rho_ref.shape, jnp.float32)
    for s in range(2):
        cpad[s, 0:comps, :] = coupling_ref[s]
        c_high, c_low = split(coulomb_ref[s])
        term = mm(rho_high, c_high) + (mm(rho_high, c_low) + mm(rho_low, c_high))
        coul = jnp.where(kind == s, 2.0 * term, coul)
    for copy in copies:
        copy.wait()
    mine = (part_ref[0] + around[0]) + (around[1] + around[2])
    total_ref[...] = mine
    parts[me] = mine
    copies = [
        remote(total_ref, parts.at[me], 2 + t, others[t - 1]) for t in range(1, bands)
    ]
    for copy in copies:
        copy.wait()
    moments = (parts[0] + parts[1]) + (parts[2] + parts[3])
    for b in range(4, bands):
        moments = moments + parts[b]
    moments = moments[:, 0 : cpad.shape[1]]
    summed = jnp.zeros(rho_ref.shape, jnp.float32)
    for s in range(2):
        term = jnp.dot(moments, cpad[s], precision=PRECISE, preferred_element_type=jnp.float32)
        summed = jnp.where(kind == s, term, summed)
    ham_ref[...] = jnp.where(live, summed + coul, 0.0)


def apply_kernel(ham_ref, proj_ref, out_ham_ref, out_ref):
    out_ham_ref[...] = ham_ref[...]
    square = NI * NI
    row, col = iota((square, square), 0), iota((square, square), 1)
    spread = (lax.rem(row, NI) == lax.rem(col, NI)).astype(jnp.bfloat16)
    same_i = lax.rem(row, NI) == col // NI
    same_a = row // NI == col // NI
    for t in range(ham_ref.shape[0] // NI):
        block = ham_ref[t * NI : (t + 1) * NI, :]
        tall = jnp.broadcast_to(block[:, None, :], (NI, NI, square)).reshape(square, square)
        high, low = split(jnp.where(same_i, tall, 0.0))
        d_high = jnp.where(same_a, mm(high, spread), 0.0).astype(jnp.bfloat16)
        d_low = jnp.where(same_a, mm(low, spread), 0.0).astype(jnp.bfloat16)
        p_high, p_low = split(proj_ref[t * square : (t + 1) * square, :])
        out_ref[t * square : (t + 1) * square, :] = mm(d_high, p_high) + (
            mm(d_high, p_low) + mm(d_low, p_high)
        )


def local(
    density, hartree, box_root, species, atom_count, shape_functions, coupling, coulomb, rho_ij, projections
):
    f32 = jnp.float32
    wx, wy, depth = density.shape
    bands = lax.axis_size("band")
    slots = box_root.shape[1]
    kinds, comps, cells = shape_functions.shape
    vmem = pl.BlockSpec(memory_space=pltpu.VMEM)
    smem = pl.BlockSpec(memory_space=pltpu.SMEM)
    species_row = species.reshape(1, slots)

    face = lambda *s: pltpu.VMEM(s, f32)
    potential, atoms = pl.pallas_call(
        grid_kernel,
        name="grid_kernel",
        out_shape=(
            jax.ShapeDtypeStruct((wx, wy, depth), f32),
            jax.ShapeDtypeStruct((2, 8, 256), jnp.int32),
        ),
        in_specs=[vmem, vmem, vmem, vmem, smem],
        out_specs=(vmem, vmem),
        scratch_shapes=[
            face(wx + 2, wy + 16, depth), face(wx + 2, wy, depth), face(wx, wy + 16, depth),
            face(wx, wy, depth), face(wx, wy, depth),
            face(2, wy, depth), face(2, wx, depth), face(wy, depth),
            face(2, wy, depth), face(2, wx, depth), face(2, wy, depth),
            face(2, wy, depth), face(2, wx, depth), face(wy, depth),
            face(2, wy, depth), face(2, wx, depth), face(2, wy, depth),
            pltpu.VMEM((8, 128), jnp.int32), pltpu.VMEM((3, 8, 128), jnp.int32),
            pltpu.SemaphoreType.DMA((15,)), pltpu.SemaphoreType.DMA((15,)),
        ],
        compiler_params=pltpu.CompilerParams(
            collective_id=0, has_side_effects=True, vmem_limit_bytes=VMEM_LIMIT
        ),
    )(density, hartree, box_root, species_row, atom_count)

    turned = shape_functions.reshape(kinds, comps, BOX * BOX, BOX)
    turned = turned.transpose(0, 1, 3, 2).reshape(kinds, comps * BOX, BOX * BOX)
    rounded = lax.reduce_precision(turned, 8, 7)
    high, low = rounded.astype(jnp.bfloat16), (turned - rounded).astype(jnp.bfloat16)
    lanes = GROUP * BOX
    potential, partial = pl.pallas_call(
        functools.partial(moment_kernel, depth * bands),
        name="moment_kernel",
        out_shape=(
            jax.ShapeDtypeStruct((wx, wy, depth), f32),
            jax.ShapeDtypeStruct((4, slots, 128), f32),
        ),
        in_specs=[smem, vmem, vmem, vmem],
        out_specs=(vmem, vmem),
        scratch_shapes=[
            face((wx + 2 * PAD) * (wy + 2 * PAD), depth),
            face(BOX * BOX, lanes), face(128, lanes), face(8 + 4 * slots, 128),
        ],
        compiler_params=pltpu.CompilerParams(vmem_limit_bytes=VMEM_LIMIT),
    )(atoms, potential, high, low)

    ham = pl.pallas_call(
        block_kernel,
        name="block_kernel",
        out_shape=jax.ShapeDtypeStruct(rho_ij.shape, f32),
        in_specs=[vmem, vmem, smem, vmem, vmem, vmem],
        out_specs=vmem,
        scratch_shapes=[
            face(3, slots, 128), face(bands, slots, 128), face(slots, 128), face(2, 32, NI * NI),
            pltpu.SemaphoreType.DMA((2 + bands,)), pltpu.SemaphoreType.DMA((2 + bands,)),
        ],
        compiler_params=pltpu.CompilerParams(
            collective_id=1, has_side_effects=True, vmem_limit_bytes=VMEM_LIMIT
        ),
    )(partial, species_row, atom_count, coupling, coulomb, rho_ij)

    width = projections.shape[2]
    ham, applied = pl.pallas_call(
        apply_kernel,
        name="apply_kernel",
        out_shape=(
            jax.ShapeDtypeStruct(rho_ij.shape, f32),
            jax.ShapeDtypeStruct((slots * NI, width), f32),
        ),
        in_specs=[vmem, vmem],
        out_specs=(vmem, vmem),
        compiler_params=pltpu.CompilerParams(vmem_limit_bytes=VMEM_LIMIT),
    )(ham, projections.reshape(slots * NI, width))
    return potential, ham, applied.reshape(slots, NI, width)


def solution(mesh):
    in_specs = (
        P("dx", "dyz", "band"),
        P("dx", "dyz", "band"),
        P(None, ("dx", "dyz")),
        P(("dx", "dyz")),
        P(("dx", "dyz")),
        P(),
        P(),
        P(),
        P(("dx", "dyz"), None),
        P(("dx", "dyz"), None, "band"),
    )
    out_specs = (P("dx", "dyz", "band"), P(("dx", "dyz"), None), P(("dx", "dyz"), None, "band"))
    return jax.shard_map(local, mesh=mesh, in_specs=in_specs, out_specs=out_specs, check_vma=False)
```

```python
import functools
import math

import jax
import jax.numpy as jnp
from jax import lax
from jax.experimental import pallas as pl
from jax.experimental.pallas import tpu as pltpu
from jax.sharding import PartitionSpec as P

BOX = 16
NI = 16
GROUP = 16
PAD = 16
GRID_H = 0.15
KAPPA = 0.804
MU_COEF = 0.2195149727645171
PRECISE = lax.Precision.HIGHEST
HALF = 0.5 / GRID_H
PREF = -0.75 * (3.0 / math.pi) ** (1.0 / 3.0)
RED = 4.0 * (3.0 * math.pi**2) ** (2.0 / 3.0)
MESH = pl.DeviceIdType.MESH
VMEM_LIMIT = 56 * 1024 * 1024


def iota(shape, dim):
    return lax.broadcasted_iota(jnp.int32, shape, dim)


def shifted(axis, step):
    size = lax.axis_size(axis)
    return lax.rem(lax.axis_index(axis) + (step + size), size)


def enter(devices):
    barrier = pltpu.get_barrier_semaphore()
    for device in devices:
        pl.semaphore_signal(barrier, inc=1, device_id=device, device_id_type=MESH)
    pl.semaphore_wait(barrier, len(devices))


def split(value):
    high = value.astype(jnp.bfloat16)
    return high, (value - high.astype(jnp.float32)).astype(jnp.bfloat16)


def mm(a, b):
    return jnp.dot(a, b, preferred_element_type=jnp.float32)


def pack_ends(ref):
    wx, wy, depth = ref.shape
    lane = iota((wy, depth), 1)
    packed = jnp.zeros((wy, depth), jnp.float32)
    for x in range(wx):
        moved = pltpu.roll(ref[x], 2 * x + 1, 1)
        packed = jnp.where((lane == 2 * x) | (lane == 2 * x + 1), moved, packed)
    return packed


def join_ends(before, after):
    lane = iota(before.shape, 1)
    depth = before.shape[1]
    return jnp.where(
        lax.rem(lane, 2) == 1, pltpu.roll(before, 1, 1), pltpu.roll(after, depth - 1, 1)
    )


def turn_shapes(shape_ref, turned, high_ref, low_ref, s):
    comps, cells = shape_ref.shape[1:]
    lane, sub = iota((8, 128), 1) // BOX, iota((8, 128), 0)
    wraps = [(lane // bit) % 2 == 1 for bit in (1, 2, 4)]
    octets = (comps + 7) // 8
    row, col = iota((cells // BOX, cells // BOX), 0), iota((cells // BOX, cells // BOX), 1)
    order = (row // 8 == col // 8) & (lax.rem(row + col, 8) == 0)
    order = order.astype(jnp.bfloat16)
    for o in range(octets):
        for t in range(cells // 128):
            here = slice(t * 128, (t + 1) * 128)
            if 8 * o + 8 <= comps:
                tile = shape_ref[s, 8 * o : 8 * o + 8, here]
            else:
                tile = jnp.broadcast_to(shape_ref[s, 8 * o : 8 * o + 1, here], (8, 128))
            tile = pltpu.roll(tile, 0, 1, stride=BOX, stride_axis=0)
            for bit, wrap in zip((1, 2, 4), wraps):
                tile = jnp.where(wrap, pltpu.roll(tile, 8 - bit, 0), tile)
            tile = pltpu.roll(tile, 0, 1, stride=BOX, stride_axis=0)
            turned[t * 8 : (t + 1) * 8, :] = tile
        block = turned[...].T
        rows = min(128, (comps - 8 * o) * BOX)
        high, low = split(block[0:rows, :])
        high_ref[s, o * 128 : o * 128 + rows, :] = mm(high, order).astype(jnp.bfloat16)
        low_ref[s, o * 128 : o * 128 + rows, :] = mm(low, order).astype(jnp.bfloat16)


def grid_kernel(
    dens_hbm, hart_hbm, shape_hbm, root_ref, species_ref, count_ref,
    pot_ref, list_ref, high_ref, low_ref,
    dens_ref, hart_ref, shape_ref, turned, local_sems,
    dpad, fxp, fyp, fz, slope_n_ref,
    send_x, send_y, send_z, recv_x, recv_y, recv_z,
    gsend_x, gsend_y, gsend_z, grecv_x, grecv_y, grecv_z,
    plan_send, plan_recv, send_sems, recv_sems,
):
    wx, wy, depth = dens_ref.shape
    loads = [
        pltpu.make_async_copy(src, dst, local_sems.at[i])
        for i, (src, dst) in enumerate(
            ((dens_hbm, dens_ref), (shape_hbm, shape_ref), (hart_hbm, hart_ref))
        )
    ]
    for load in loads:
        load.start()
    up_x, down_x = {"dx": shifted("dx", 1)}, {"dx": shifted("dx", -1)}
    up_y, down_y = {"dyz": shifted("dyz", 1)}, {"dyz": shifted("dyz", -1)}
    up_z, down_z = {"band": shifted("band", 1)}, {"band": shifted("band", -1)}
    up_xy = {"dx": shifted("dx", 1), "dyz": shifted("dyz", 1)}
    down_xy = {"dx": shifted("dx", -1), "dyz": shifted("dyz", -1)}
    slots = root_ref.shape[1]

    def remote(src, dst, sem, device):
        copy = pltpu.make_async_remote_copy(
            src_ref=src, dst_ref=dst, send_sem=send_sems.at[sem], recv_sem=recv_sems.at[sem],
            device_id=device, device_id_type=MESH,
        )
        copy.start()
        return copy

    loads[0].wait()
    send_x[0] = dens_ref[wx - 1]
    send_x[1] = dens_ref[0]
    send_y[0] = dens_ref[:, wy - 1, :]
    send_y[1] = dens_ref[:, 0, :]
    send_z[...] = pack_ends(dens_ref)
    plan_send[...] = jnp.zeros_like(plan_send)
    plan_send[0:1, 0:slots] = root_ref[0:1, :] - lax.axis_index("dx") * wx
    plan_send[1:2, 0:slots] = root_ref[1:2, :] - lax.axis_index("dyz") * wy
    plan_send[2:3, 0:slots] = root_ref[2:3, :]
    plan_send[3:4, 0:slots] = species_ref[...]
    plan_send[4:5, :] = jnp.full((1, 128), count_ref[0], jnp.int32)

    enter([up_x, down_x, up_y, down_y, up_z, down_z, up_xy, down_xy])
    first = [
        remote(send_z, recv_z.at[0], 0, up_z),
        remote(send_z, recv_z.at[1], 1, down_z),
        remote(send_y.at[0], recv_y.at[0], 2, up_y),
        remote(send_y.at[1], recv_y.at[1], 3, down_y),
        remote(send_x.at[0], recv_x.at[0], 4, up_x),
        remote(send_x.at[1], recv_x.at[1], 5, down_x),
    ]
    plans = [
        remote(plan_send, plan_recv.at[0], 6, up_x),
        remote(plan_send, plan_recv.at[1], 7, up_y),
        remote(plan_send, plan_recv.at[2], 8, up_xy),
    ]
    dpad[1 : wx + 1, 8 : wy + 8, :] = dens_ref[...]
    loads[1].wait()
    turn_shapes(shape_ref, turned, high_ref, low_ref, 0)
    for copy in first:
        copy.wait()
    dpad[0, 8 : wy + 8, :] = recv_x[0]
    dpad[wx + 1, 8 : wy + 8, :] = recv_x[1]
    dpad[1 : wx + 1, 7, :] = recv_y[0]
    dpad[1 : wx + 1, wy + 8, :] = recv_y[1]
    ends = join_ends(recv_z[0], recv_z[1])
    lane = iota((wy, depth), 1)

    def flux_step(x):
        here = dpad[x + 1, 8 : wy + 8, :]
        gx = (dpad[x + 2, 8 : wy + 8, :] - dpad[x, 8 : wy + 8, :]) * HALF
        gy = (dpad[x + 1, 9 : wy + 9, :] - dpad[x + 1, 7 : wy + 7, :]) * HALF
        end = pltpu.roll(ends, depth - 1 - 2 * x, 1)
        after = jnp.where(lane == depth - 1, end, pltpu.roll(here, depth - 1, 1))
        before = jnp.where(lane == 0, end, pltpu.roll(here, 1, 1))
        gz = (after - before) * HALF
        sigma = gx * gx + gy * gy + gz * gz
        log_n = jnp.log(here)
        cube = jnp.exp(log_n * (1.0 / 3.0))
        power = here * cube
        scaled = RED * power * power
        summed = scaled + (MU_COEF / KAPPA) * sigma
        both = 1.0 / (power * summed)
        u = scaled * power * both
        slope_s = (PREF / RED * MU_COEF) * u * u * (summed * both)
        slope_n_ref[x] = (4.0 / 3.0 * PREF) * cube * (1.0 + KAPPA - KAPPA * u * (3.0 - 2.0 * u))
        fxp[x + 1] = slope_s * gx
        fyp[x, 8 : wy + 8, :] = slope_s * gy
        fz[x] = slope_s * gz

    per = 4

    def flux_steps(t, carry):
        for k in range(per):
            flux_step(t * per + k)
        return carry

    lax.fori_loop(0, wx // per, flux_steps, 0)

    gsend_x[0] = fxp[wx]
    gsend_x[1] = fxp[1]
    gsend_y[0] = fyp[:, wy + 7, :]
    gsend_y[1] = fyp[:, 8, :]
    gsend_z[...] = pack_ends(fz)
    second = [
        remote(gsend_z, grecv_z.at[0], 9, up_z),
        remote(gsend_z, grecv_z.at[1], 10, down_z),
        remote(gsend_y.at[0], grecv_y.at[0], 11, up_y),
        remote(gsend_y.at[1], grecv_y.at[1], 12, down_y),
        remote(gsend_x.at[0], grecv_x.at[0], 13, up_x),
        remote(gsend_x.at[1], grecv_x.at[1], 14, down_x),
    ]

    for copy in plans:
        copy.wait()
    depth_all = depth * lax.axis_size("band")
    first_z = lax.axis_index("band") * depth
    columns = []
    for c in range(4):
        plan = plan_send[...] if c == 0 else plan_recv[c - 1]
        x = plan[0:1, :] - (wx if c in (1, 3) else 0)
        y = plan[1:2, :] - (wy if c in (2, 3) else 0)
        z = plan[2:3, :] - first_z
        z = jnp.where(z < 0, z + depth_all, z)
        slot = iota((1, 128), 1)
        meets = (slot < plan[4:5, :]) & (slot < slots)
        meets &= (x > -BOX) & (y > -BOX) & (x < wx) & (y < wy)
        meets &= (z < depth) | (z > depth_all - BOX)
        rows = (x + PAD) * (wy + 2 * PAD) + (y + PAD)
        dest = 8 + c * slots + slot
        columns.append([v.astype(jnp.int32) for v in (meets, rows, z, dest, plan[3:4, :])])
    left = iota((1, 128), 1) < slots
    merged = []
    for f in range(5):
        halves = [
            jnp.where(left, columns[c][f], pltpu.roll(columns[c + 1][f], slots, 1)) for c in (0, 2)
        ]
        merged.append(jnp.concatenate(halves, 1))
    meets, rows, z, dest, kind = merged
    wide = 256
    upper = (iota((wide, wide), 0) <= iota((wide, wide), 1)).astype(jnp.bfloat16)
    row8 = iota((8, wide), 0)
    picked = jnp.where((meets == 1) & (kind == row8), 1.0, 0.0)
    order = mm(picked.astype(jnp.bfloat16), upper)
    place = iota((wide, wide), 0).astype(jnp.float32) + 1.0
    fields = jnp.where(row8 == 0, rows, jnp.where(row8 == 1, z, jnp.where(row8 == 2, dest, 0)))
    f_high, f_low = split(fields.astype(jnp.float32))
    across = (((1,), (1,)), ((), ()))
    for s in range(2):
        total = jnp.sum(picked[s : s + 1, :], axis=1, keepdims=True)
        spot = jnp.where(picked[s : s + 1, :] > 0.5, order[s : s + 1, :], 0.0)
        onehot = (spot == place).astype(jnp.bfloat16)
        got = lax.dot_general(f_high, onehot, across, preferred_element_type=jnp.float32)
        got = got + lax.dot_general(f_low, onehot, across, preferred_element_type=jnp.float32)
        got = jnp.where(row8 == 3, total, got)
        list_ref[s] = (got + 0.5).astype(jnp.int32)
    turn_shapes(shape_ref, turned, high_ref, low_ref, 1)

    loads[2].wait()
    for copy in second:
        copy.wait()
    fxp[0] = grecv_x[0]
    fxp[wx + 1] = grecv_x[1]
    fyp[:, 7, :] = grecv_y[0]
    fyp[:, wy + 8, :] = grecv_y[1]
    flux_ends = join_ends(grecv_z[0], grecv_z[1])

    def pot_step(x):
        here = fz[x]
        end = pltpu.roll(flux_ends, depth - 1 - 2 * x, 1)
        after = jnp.where(lane == depth - 1, end, pltpu.roll(here, depth - 1, 1))
        before = jnp.where(lane == 0, end, pltpu.roll(here, 1, 1))
        spread = (fxp[x + 2] - fxp[x]) * HALF
        spread = spread + (fyp[x, 9 : wy + 9, :] - fyp[x, 7 : wy + 7, :]) * HALF
        spread = spread + (after - before) * HALF
        pot_ref[x] = hart_ref[x] + slope_n_ref[x] - 2.0 * spread

    def pot_steps(t, carry):
        for k in range(per):
            pot_step(t * per + k)
        return carry

    lax.fori_loop(0, wx // per, pot_steps, 0)


def moment_kernel(
    depth_all, list_ref, pot_ref, high_ref, low_ref, out_pot_ref, out_ref, padded, gathered, folded, sums
):
    wx, wy, depth = pot_ref.shape
    rows_y = wy + 2 * PAD
    comps = high_ref.shape[1] // BOX
    out_pot_ref[...] = pot_ref[...]
    padded[...] = jnp.zeros_like(padded)
    for x in range(wx):
        start = (x + PAD) * rows_y + PAD
        padded[start : start + wy, :] = pot_ref[x]
    sums[...] = jnp.zeros_like(sums)
    folded[...] = jnp.zeros_like(folded)
    lanes = GROUP * BOX
    per_tile = 128 // BOX
    lane = iota((BOX, 128), 1)
    adder = (iota((GROUP, lanes), 0) == iota((GROUP, lanes), 1) // BOX).astype(jnp.float32)
    keep = lax.rem(iota((BOX, lanes), 1), BOX) == iota((BOX, lanes), 0)

    for s in range(2):
        total = list_ref[s, 3, 0]

        def one_group(g, carry, s=s, total=total):
            for tile in range(lanes // 128):
                first = g * GROUP + tile * per_tile
                across = slice(tile * 128, (tile + 1) * 128)

                @pl.when(first < total)
                def _(first=first, across=across):
                    plan = []
                    for q in range(per_tile):
                        left = q * BOX
                        z = list_ref[s, 1, first + q]
                        shift = lax.rem(left + depth_all - z, depth)
                        cell = z + lane - left
                        cell = jnp.where(cell >= depth_all, cell - depth_all, cell)
                        mine = (lane >= left) & (lane < left + BOX) & (cell < depth)
                        plan.append((list_ref[s, 0, first + q], shift, mine))
                    for i in range(BOX):
                        made = jnp.zeros((BOX, 128), jnp.float32)
                        for row, shift, mine in plan:
                            piece = padded[pl.ds(row + i * rows_y, BOX), :]
                            made = jnp.where(mine, pltpu.roll(piece, shift, 1), made)
                        gathered[i * BOX : (i + 1) * BOX, across] = made

                @pl.when(first >= total)
                def _(across=across):
                    gathered[:, across] = jnp.zeros((BOX * BOX, 128), jnp.float32)

            g_high, g_low = split(gathered[...])
            product = mm(high_ref[s], g_high) + (mm(high_ref[s], g_low) + mm(low_ref[s], g_high))
            product = jnp.where(keep[None], product.reshape(comps, BOX, lanes), 0.0)
            folded[0:comps, :] = jnp.sum(product, axis=1)
            result = lax.dot_general(
                adder, folded[...], (((1,), (1,)), ((), ())), precision=PRECISE,
                preferred_element_type=jnp.float32,
            ) * (GRID_H**3)
            for q in range(GROUP):
                spot = list_ref[s, 2, g * GROUP + q]
                sums[pl.ds(spot, 1), :] = result[q : q + 1, :]
            return carry

        lax.fori_loop(0, (total + GROUP - 1) // GROUP, one_group, 0)
    slots = out_ref.shape[1]
    for c in range(4):
        out_ref[c] = sums[8 + c * slots : 8 + (c + 1) * slots, :]


def block_kernel(
    part_ref, species_ref, count_ref, coupling_ref, coulomb_ref, rho_ref, ham_ref,
    around, parts, total_ref, cpad, send_sems, recv_sems,
):
    bands = lax.axis_size("band")
    me = lax.axis_index("band")
    slots = part_ref.shape[1]
    up_x, down_x = {"dx": shifted("dx", 1)}, {"dx": shifted("dx", -1)}
    up_y, down_y = {"dyz": shifted("dyz", 1)}, {"dyz": shifted("dyz", -1)}
    up_xy = {"dx": shifted("dx", 1), "dyz": shifted("dyz", 1)}
    down_xy = {"dx": shifted("dx", -1), "dyz": shifted("dyz", -1)}
    others = [{"band": shifted("band", t)} for t in range(1, bands)]
    enter([up_x, down_x, up_y, down_y, up_xy, down_xy] + others)

    def remote(src, dst, sem, device):
        copy = pltpu.make_async_remote_copy(
            src_ref=src, dst_ref=dst, send_sem=send_sems.at[sem], recv_sem=recv_sems.at[sem],
            device_id=device, device_id_type=MESH,
        )
        copy.start()
        return copy

    copies = [
        remote(part_ref.at[c + 1], around.at[c], c, device)
        for c, device in enumerate((down_x, down_y, down_xy))
    ]
    eye = iota((slots, slots), 0) == iota((slots, slots), 1)
    kind = jnp.sum(jnp.where(eye, species_ref[...], 0), axis=1, keepdims=True)
    live = iota((slots, 1), 0) < count_ref[0]
    cpad[...] = jnp.zeros_like(cpad)
    comps = coupling_ref.shape[1]
    rho_high, rho_low = split(rho_ref[...])
    coul = jnp.zeros(rho_ref.shape, jnp.float32)
    for s in range(2):
        cpad[s, 0:comps, :] = coupling_ref[s]
        c_high, c_low = split(coulomb_ref[s])
        term = mm(rho_high, c_high) + (mm(rho_high, c_low) + mm(rho_low, c_high))
        coul = jnp.where(kind == s, 2.0 * term, coul)
    for copy in copies:
        copy.wait()
    mine = (part_ref[0] + around[0]) + (around[1] + around[2])
    total_ref[...] = mine
    parts[me] = mine
    copies = [
        remote(total_ref, parts.at[me], 2 + t, others[t - 1]) for t in range(1, bands)
    ]
    for copy in copies:
        copy.wait()
    moments = (parts[0] + parts[1]) + (parts[2] + parts[3])
    for b in range(4, bands):
        moments = moments + parts[b]
    moments = moments[:, 0 : cpad.shape[1]]
    summed = jnp.zeros(rho_ref.shape, jnp.float32)
    for s in range(2):
        term = jnp.dot(moments, cpad[s], precision=PRECISE, preferred_element_type=jnp.float32)
        summed = jnp.where(kind == s, term, summed)
    ham_ref[...] = jnp.where(live, summed + coul, 0.0)


def apply_kernel(ham_ref, proj_ref, out_ham_ref, out_ref):
    out_ham_ref[...] = ham_ref[...]
    square = NI * NI
    row, col = iota((square, square), 0), iota((square, square), 1)
    spread = (lax.rem(row, NI) == lax.rem(col, NI)).astype(jnp.bfloat16)
    same_i = lax.rem(row, NI) == col // NI
    same_a = row // NI == col // NI
    for t in range(ham_ref.shape[0] // NI):
        block = ham_ref[t * NI : (t + 1) * NI, :]
        tall = jnp.broadcast_to(block[:, None, :], (NI, NI, square)).reshape(square, square)
        high, low = split(jnp.where(same_i, tall, 0.0))
        d_high = jnp.where(same_a, mm(high, spread), 0.0).astype(jnp.bfloat16)
        d_low = jnp.where(same_a, mm(low, spread), 0.0).astype(jnp.bfloat16)
        p_high, p_low = split(proj_ref[t * square : (t + 1) * square, :])
        out_ref[t * square : (t + 1) * square, :] = mm(d_high, p_high) + (
            mm(d_high, p_low) + mm(d_low, p_high)
        )


def local(
    density, hartree, box_root, species, atom_count, shape_functions, coupling, coulomb, rho_ij, projections
):
    f32 = jnp.float32
    wx, wy, depth = density.shape
    bands = lax.axis_size("band")
    slots = box_root.shape[1]
    kinds, comps, cells = shape_functions.shape
    vmem = pl.BlockSpec(memory_space=pltpu.VMEM)
    anywhere = pl.BlockSpec(memory_space=pl.ANY)
    smem = pl.BlockSpec(memory_space=pltpu.SMEM)
    species_row = species.reshape(1, slots)

    face = lambda *s: pltpu.VMEM(s, f32)
    turned_shape = jax.ShapeDtypeStruct((kinds, comps * BOX, BOX * BOX), jnp.bfloat16)
    potential, atoms, high, low = pl.pallas_call(
        grid_kernel,
        name="grid_kernel",
        out_shape=(
            jax.ShapeDtypeStruct((wx, wy, depth), f32),
            jax.ShapeDtypeStruct((2, 8, 256), jnp.int32),
            turned_shape,
            turned_shape,
        ),
        in_specs=[anywhere, anywhere, anywhere, vmem, vmem, smem],
        out_specs=(vmem,) * 4,
        scratch_shapes=[
            face(wx, wy, depth), face(wx, wy, depth), face(kinds, comps, cells),
            face(BOX * BOX, 128), pltpu.SemaphoreType.DMA((3,)),
            face(wx + 2, wy + 16, depth), face(wx + 2, wy, depth), face(wx, wy + 16, depth),
            face(wx, wy, depth), face(wx, wy, depth),
            face(2, wy, depth), face(2, wx, depth), face(wy, depth),
            face(2, wy, depth), face(2, wx, depth), face(2, wy, depth),
            face(2, wy, depth), face(2, wx, depth), face(wy, depth),
            face(2, wy, depth), face(2, wx, depth), face(2, wy, depth),
            pltpu.VMEM((8, 128), jnp.int32), pltpu.VMEM((3, 8, 128), jnp.int32),
            pltpu.SemaphoreType.DMA((15,)), pltpu.SemaphoreType.DMA((15,)),
        ],
        compiler_params=pltpu.CompilerParams(
            collective_id=0, has_side_effects=True, vmem_limit_bytes=VMEM_LIMIT
        ),
    )(density, hartree, shape_functions, box_root, species_row, atom_count)

    lanes = GROUP * BOX
    potential, partial = pl.pallas_call(
        functools.partial(moment_kernel, depth * bands),
        name="moment_kernel",
        out_shape=(
            jax.ShapeDtypeStruct((wx, wy, depth), f32),
            jax.ShapeDtypeStruct((4, slots, 128), f32),
        ),
        in_specs=[smem, vmem, vmem, vmem],
        out_specs=(vmem, vmem),
        scratch_shapes=[
            face((wx + 2 * PAD) * (wy + 2 * PAD), depth),
            face(BOX * BOX, lanes), face(128, lanes), face(8 + 4 * slots, 128),
        ],
        compiler_params=pltpu.CompilerParams(vmem_limit_bytes=VMEM_LIMIT),
    )(atoms, potential, high, low)

    ham = pl.pallas_call(
        block_kernel,
        name="block_kernel",
        out_shape=jax.ShapeDtypeStruct(rho_ij.shape, f32),
        in_specs=[vmem, vmem, smem, vmem, vmem, vmem],
        out_specs=vmem,
        scratch_shapes=[
            face(3, slots, 128), face(bands, slots, 128), face(slots, 128), face(2, 32, NI * NI),
            pltpu.SemaphoreType.DMA((2 + bands,)), pltpu.SemaphoreType.DMA((2 + bands,)),
        ],
        compiler_params=pltpu.CompilerParams(
            collective_id=1, has_side_effects=True, vmem_limit_bytes=VMEM_LIMIT
        ),
    )(partial, species_row, atom_count, coupling, coulomb, rho_ij)

    width = projections.shape[2]
    ham, applied = pl.pallas_call(
        apply_kernel,
        name="apply_kernel",
        out_shape=(
            jax.ShapeDtypeStruct(rho_ij.shape, f32),
            jax.ShapeDtypeStruct((slots * NI, width), f32),
        ),
        in_specs=[vmem, vmem],
        out_specs=(vmem, vmem),
        compiler_params=pltpu.CompilerParams(vmem_limit_bytes=VMEM_LIMIT),
    )(ham, projections.reshape(slots * NI, width))
    return potential, ham, applied.reshape(slots, NI, width)


def solution(mesh):
    in_specs = (
        P("dx", "dyz", "band"),
        P("dx", "dyz", "band"),
        P(None, ("dx", "dyz")),
        P(("dx", "dyz")),
        P(("dx", "dyz")),
        P(),
        P(),
        P(),
        P(("dx", "dyz"), None),
        P(("dx", "dyz"), None, "band"),
    )
    out_specs = (P("dx", "dyz", "band"), P(("dx", "dyz"), None), P(("dx", "dyz"), None, "band"))
    return jax.shard_map(local, mesh=mesh, in_specs=in_specs, out_specs=out_specs, check_vma=False)
```

```python
import functools
import math

import jax
import jax.numpy as jnp
from jax import lax
from jax.experimental import pallas as pl
from jax.experimental.pallas import tpu as pltpu
from jax.sharding import PartitionSpec as P

BOX = 16
NI = 16
GROUP = 16
LANES = 32
PAD = 16
GRID_H = 0.15
KAPPA = 0.804
MU_COEF = 0.2195149727645171
PRECISE = lax.Precision.HIGHEST
HALF = 0.5 / GRID_H
PREF = -0.75 * (3.0 / math.pi) ** (1.0 / 3.0)
RED = 4.0 * (3.0 * math.pi**2) ** (2.0 / 3.0)
MESH = pl.DeviceIdType.MESH
VMEM_LIMIT = 20 * 1024 * 1024


def iota(shape, dim):
    return lax.broadcasted_iota(jnp.int32, shape, dim)


def shifted(axis, step):
    size = lax.axis_size(axis)
    return lax.rem(lax.axis_index(axis) + (step + size), size)


def enter(devices):
    barrier = pltpu.get_barrier_semaphore()
    for device in devices:
        pl.semaphore_signal(barrier, inc=1, device_id=device, device_id_type=MESH)
    pl.semaphore_wait(barrier, len(devices))


def split(value):
    high = value.astype(jnp.bfloat16)
    return high, (value - high.astype(jnp.float32)).astype(jnp.bfloat16)


def mm(a, b):
    return jnp.dot(a, b, preferred_element_type=jnp.float32)


def pack_ends(ref):
    wx, wy, depth = ref.shape
    lane = iota((wy, depth), 1)
    packed = jnp.zeros((wy, depth), jnp.float32)
    for x in range(wx):
        moved = pltpu.roll(ref[x], 2 * x + 1, 1)
        packed = jnp.where((lane == 2 * x) | (lane == 2 * x + 1), moved, packed)
    return packed


def join_ends(before, after):
    lane = iota(before.shape, 1)
    depth = before.shape[1]
    return jnp.where(
        lax.rem(lane, 2) == 1, pltpu.roll(before, 1, 1), pltpu.roll(after, depth - 1, 1)
    )


def turn_shapes(shape_ref, turned, high_ref, low_ref, s):
    comps, cells = shape_ref.shape[1:]
    lane, sub = iota((8, 128), 1) // BOX, iota((8, 128), 0)
    wraps = [(lane // bit) % 2 == 1 for bit in (1, 2, 4)]
    octets = (comps + 7) // 8
    row, col = iota((cells // BOX, cells // BOX), 0), iota((cells // BOX, cells // BOX), 1)
    order = (row // 8 == col // 8) & (lax.rem(row + col, 8) == 0)
    order = order.astype(jnp.bfloat16)
    for o in range(octets):
        for t in range(cells // 128):
            here = slice(t * 128, (t + 1) * 128)
            if 8 * o + 8 <= comps:
                tile = shape_ref[s, 8 * o : 8 * o + 8, here]
            else:
                tile = jnp.broadcast_to(shape_ref[s, 8 * o : 8 * o + 1, here], (8, 128))
            tile = pltpu.roll(tile, 0, 1, stride=BOX, stride_axis=0)
            for bit, wrap in zip((1, 2, 4), wraps):
                tile = jnp.where(wrap, pltpu.roll(tile, 8 - bit, 0), tile)
            tile = pltpu.roll(tile, 0, 1, stride=BOX, stride_axis=0)
            turned[t * 8 : (t + 1) * 8, :] = tile
        block = turned[...].T
        rows = min(128, (comps - 8 * o) * BOX)
        high, low = split(block[0:rows, :])
        high_ref[s, o * 128 : o * 128 + rows, :] = mm(high, order).astype(jnp.bfloat16)
        low_ref[s, o * 128 : o * 128 + rows, :] = mm(low, order).astype(jnp.bfloat16)


def grid_kernel(
    dens_hbm, hart_hbm, shape_hbm, root_ref, species_ref, count_ref,
    pot_ref, list_ref, high_ref, low_ref,
    dens_ref, hart_ref, shape_ref, turned, local_sems,
    dpad, fxp, fyp, fz, slope_n_ref,
    send_x, send_y, send_z, recv_x, recv_y, recv_z,
    gsend_x, gsend_y, gsend_z, grecv_x, grecv_y, grecv_z,
    plan_send, plan_recv, send_sems, recv_sems,
):
    wx, wy, depth = dens_ref.shape
    loads = [
        pltpu.make_async_copy(src, dst, local_sems.at[i])
        for i, (src, dst) in enumerate(
            (
                (dens_hbm, dens_ref),
                (shape_hbm.at[:, 0, :], shape_ref.at[0]),
                (shape_hbm.at[:, 1, :], shape_ref.at[1]),
                (hart_hbm, hart_ref),
            )
        )
    ]
    for load in loads:
        load.start()
    up_x, down_x = {"dx": shifted("dx", 1)}, {"dx": shifted("dx", -1)}
    up_y, down_y = {"dyz": shifted("dyz", 1)}, {"dyz": shifted("dyz", -1)}
    up_z, down_z = {"band": shifted("band", 1)}, {"band": shifted("band", -1)}
    up_xy = {"dx": shifted("dx", 1), "dyz": shifted("dyz", 1)}
    down_xy = {"dx": shifted("dx", -1), "dyz": shifted("dyz", -1)}
    slots = root_ref.shape[1]

    def remote(src, dst, sem, device):
        copy = pltpu.make_async_remote_copy(
            src_ref=src, dst_ref=dst, send_sem=send_sems.at[sem], recv_sem=recv_sems.at[sem],
            device_id=device, device_id_type=MESH,
        )
        copy.start()
        return copy

    loads[0].wait()
    send_x[0] = dens_ref[wx - 1]
    send_x[1] = dens_ref[0]
    send_y[0] = dens_ref[:, wy - 1, :]
    send_y[1] = dens_ref[:, 0, :]
    send_z[...] = pack_ends(dens_ref)
    plan_send[...] = jnp.zeros_like(plan_send)
    plan_send[0:1, 0:slots] = root_ref[0:1, :] - lax.axis_index("dx") * wx
    plan_send[1:2, 0:slots] = root_ref[1:2, :] - lax.axis_index("dyz") * wy
    plan_send[2:3, 0:slots] = root_ref[2:3, :]
    plan_send[3:4, 0:slots] = species_ref[...]
    plan_send[4:5, :] = jnp.full((1, 128), count_ref[0], jnp.int32)

    enter([up_x, down_x, up_y, down_y, up_z, down_z, up_xy, down_xy])
    first = [
        remote(send_z, recv_z.at[0], 0, up_z),
        remote(send_z, recv_z.at[1], 1, down_z),
        remote(send_y.at[0], recv_y.at[0], 2, up_y),
        remote(send_y.at[1], recv_y.at[1], 3, down_y),
        remote(send_x.at[0], recv_x.at[0], 4, up_x),
        remote(send_x.at[1], recv_x.at[1], 5, down_x),
    ]
    plans = [
        remote(plan_send, plan_recv.at[0], 6, up_x),
        remote(plan_send, plan_recv.at[1], 7, up_y),
        remote(plan_send, plan_recv.at[2], 8, up_xy),
    ]
    dpad[1 : wx + 1, 8 : wy + 8, :] = dens_ref[...]
    loads[1].wait()
    turn_shapes(shape_ref, turned, high_ref, low_ref, 0)
    for copy in first:
        copy.wait()
    dpad[0, 8 : wy + 8, :] = recv_x[0]
    dpad[wx + 1, 8 : wy + 8, :] = recv_x[1]
    dpad[1 : wx + 1, 7, :] = recv_y[0]
    dpad[1 : wx + 1, wy + 8, :] = recv_y[1]
    ends = join_ends(recv_z[0], recv_z[1])
    lane = iota((wy, depth), 1)

    def flux_step(x):
        here = dpad[x + 1, 8 : wy + 8, :]
        gx = (dpad[x + 2, 8 : wy + 8, :] - dpad[x, 8 : wy + 8, :]) * HALF
        gy = (dpad[x + 1, 9 : wy + 9, :] - dpad[x + 1, 7 : wy + 7, :]) * HALF
        end = pltpu.roll(ends, depth - 1 - 2 * x, 1)
        after = jnp.where(lane == depth - 1, end, pltpu.roll(here, depth - 1, 1))
        before = jnp.where(lane == 0, end, pltpu.roll(here, 1, 1))
        gz = (after - before) * HALF
        sigma = gx * gx + gy * gy + gz * gz
        log_n = jnp.log(here)
        cube = jnp.exp(log_n * (1.0 / 3.0))
        power = here * cube
        scaled = RED * power * power
        summed = scaled + (MU_COEF / KAPPA) * sigma
        both = 1.0 / (power * summed)
        u = scaled * power * both
        slope_s = (PREF / RED * MU_COEF) * u * u * (summed * both)
        slope_n_ref[x] = (4.0 / 3.0 * PREF) * cube * (1.0 + KAPPA - KAPPA * u * (3.0 - 2.0 * u))
        fxp[x + 1] = slope_s * gx
        fyp[x, 8 : wy + 8, :] = slope_s * gy
        fz[x] = slope_s * gz

    per = 4

    def flux_steps(t, carry):
        for k in range(per):
            flux_step(t * per + k)
        return carry

    lax.fori_loop(0, wx // per, flux_steps, 0)

    gsend_x[0] = fxp[wx]
    gsend_x[1] = fxp[1]
    gsend_y[0] = fyp[:, wy + 7, :]
    gsend_y[1] = fyp[:, 8, :]
    gsend_z[...] = pack_ends(fz)
    second = [
        remote(gsend_z, grecv_z.at[0], 9, up_z),
        remote(gsend_z, grecv_z.at[1], 10, down_z),
        remote(gsend_y.at[0], grecv_y.at[0], 11, up_y),
        remote(gsend_y.at[1], grecv_y.at[1], 12, down_y),
        remote(gsend_x.at[0], grecv_x.at[0], 13, up_x),
        remote(gsend_x.at[1], grecv_x.at[1], 14, down_x),
    ]

    for copy in plans:
        copy.wait()
    depth_all = depth * lax.axis_size("band")
    first_z = lax.axis_index("band") * depth
    columns = []
    for c in range(4):
        plan = plan_send[...] if c == 0 else plan_recv[c - 1]
        x = plan[0:1, :] - (wx if c in (1, 3) else 0)
        y = plan[1:2, :] - (wy if c in (2, 3) else 0)
        z = plan[2:3, :] - first_z
        z = jnp.where(z < 0, z + depth_all, z)
        slot = iota((1, 128), 1)
        meets = (slot < plan[4:5, :]) & (slot < slots)
        meets &= (x > -BOX) & (y > -BOX) & (x < wx) & (y < wy)
        meets &= (z < depth) | (z > depth_all - BOX)
        rows = (x + PAD) * (wy + 2 * PAD) + (y + PAD)
        dest = 8 + c * slots + slot
        columns.append([v.astype(jnp.int32) for v in (meets, rows, z, dest, plan[3:4, :])])
    left = iota((1, 128), 1) < slots
    merged = []
    for f in range(5):
        halves = [
            jnp.where(left, columns[c][f], pltpu.roll(columns[c + 1][f], slots, 1)) for c in (0, 2)
        ]
        merged.append(jnp.concatenate(halves, 1))
    meets, rows, z, dest, kind = merged
    wide = 256
    upper = (iota((wide, wide), 0) <= iota((wide, wide), 1)).astype(jnp.bfloat16)
    row8 = iota((8, wide), 0)
    picked = jnp.where((meets == 1) & (kind == row8), 1.0, 0.0)
    order = mm(picked.astype(jnp.bfloat16), upper)
    place = iota((wide, wide), 0).astype(jnp.float32) + 1.0
    fields = jnp.where(row8 == 0, rows, jnp.where(row8 == 1, z, jnp.where(row8 == 2, dest, 0)))
    f_high, f_low = split(fields.astype(jnp.float32))
    across = (((1,), (1,)), ((), ()))
    for s in range(2):
        total = jnp.sum(picked[s : s + 1, :], axis=1, keepdims=True)
        spot = jnp.where(picked[s : s + 1, :] > 0.5, order[s : s + 1, :], 0.0)
        onehot = (spot == place).astype(jnp.bfloat16)
        got = lax.dot_general(f_high, onehot, across, preferred_element_type=jnp.float32)
        got = got + lax.dot_general(f_low, onehot, across, preferred_element_type=jnp.float32)
        got = jnp.where(row8 == 3, total, got)
        list_ref[s] = (got + 0.5).astype(jnp.int32)
    loads[2].wait()
    turn_shapes(shape_ref, turned, high_ref, low_ref, 1)

    loads[3].wait()
    for copy in second:
        copy.wait()
    fxp[0] = grecv_x[0]
    fxp[wx + 1] = grecv_x[1]
    fyp[:, 7, :] = grecv_y[0]
    fyp[:, wy + 8, :] = grecv_y[1]
    flux_ends = join_ends(grecv_z[0], grecv_z[1])

    def pot_step(x):
        here = fz[x]
        end = pltpu.roll(flux_ends, depth - 1 - 2 * x, 1)
        after = jnp.where(lane == depth - 1, end, pltpu.roll(here, depth - 1, 1))
        before = jnp.where(lane == 0, end, pltpu.roll(here, 1, 1))
        spread = (fxp[x + 2] - fxp[x]) * HALF
        spread = spread + (fyp[x, 9 : wy + 9, :] - fyp[x, 7 : wy + 7, :]) * HALF
        spread = spread + (after - before) * HALF
        pot_ref[x] = hart_ref[x] + slope_n_ref[x] - 2.0 * spread

    def pot_steps(t, carry):
        for k in range(per):
            pot_step(t * per + k)
        return carry

    lax.fori_loop(0, wx // per, pot_steps, 0)


def moment_kernel(
    depth_all, list_ref, pot_ref, high_ref, low_ref, out_pot_ref, out_ref, padded, gathered, folded, sums, sem
):
    wx, wy, depth = pot_ref.shape
    rows_y = wy + 2 * PAD
    comps = high_ref.shape[1] // BOX
    store = pltpu.make_async_copy(pot_ref, out_pot_ref, sem)
    store.start()
    padded[...] = jnp.zeros_like(padded)
    for x in range(wx):
        start = (x + PAD) * rows_y + PAD
        padded[start : start + wy, :] = pot_ref[x]
    sums[...] = jnp.zeros_like(sums)
    folded[...] = jnp.zeros_like(folded)
    lanes = GROUP * BOX
    per_tile = 128 // BOX
    lane = iota((BOX, 128), 1)
    adder = (iota((GROUP, lanes), 0) == iota((GROUP, lanes), 1) // BOX).astype(jnp.float32)
    keep = lax.rem(iota((BOX, lanes), 1), BOX) == iota((BOX, lanes), 0)

    for s in range(2):
        total = list_ref[s, 3, 0]

        def one_group(g, carry, s=s, total=total):
            for tile in range(lanes // 128):
                first = g * GROUP + tile * per_tile
                across = slice(tile * 128, (tile + 1) * 128)

                @pl.when(first < total)
                def _(first=first, across=across):
                    plan = []
                    for q in range(per_tile):
                        left = q * BOX
                        z = list_ref[s, 1, first + q]
                        shift = lax.rem(left + depth_all - z, depth)
                        cell = z + lane - left
                        cell = jnp.where(cell >= depth_all, cell - depth_all, cell)
                        mine = (lane >= left) & (lane < left + BOX) & (cell < depth)
                        plan.append((list_ref[s, 0, first + q], shift, mine))
                    for i in range(BOX):
                        made = jnp.zeros((BOX, 128), jnp.float32)
                        for row, shift, mine in plan:
                            piece = padded[pl.ds(row + i * rows_y, BOX), :]
                            made = jnp.where(mine, pltpu.roll(piece, shift, 1), made)
                        gathered[i * BOX : (i + 1) * BOX, across] = made

                @pl.when(first >= total)
                def _(across=across):
                    gathered[:, across] = jnp.zeros((BOX * BOX, 128), jnp.float32)

            g_high, g_low = split(gathered[...])
            product = mm(high_ref[s], g_high) + (mm(high_ref[s], g_low) + mm(low_ref[s], g_high))
            product = jnp.where(keep[None], product.reshape(comps, BOX, lanes), 0.0)
            folded[0:comps, :] = jnp.sum(product, axis=1)
            result = lax.dot_general(
                adder, folded[...], (((1,), (1,)), ((), ())), precision=PRECISE,
                preferred_element_type=jnp.float32,
            ) * (GRID_H**3)
            for q in range(GROUP):
                spot = list_ref[s, 2, g * GROUP + q]
                sums[pl.ds(spot, 1), :] = result[q : q + 1, :]
            return carry

        lax.fori_loop(0, (total + GROUP - 1) // GROUP, one_group, 0)
    slots = (sums.shape[0] - 8) // 4
    for c in range(4):
        held = jnp.zeros(out_ref.shape[1:], jnp.float32)
        for r in range(slots // GROUP):
            start = 8 + c * slots + r * GROUP
            held = held + pltpu.roll(sums[start : start + GROUP, :], r * LANES, 1)
        out_ref[c] = held
    store.wait()


def block_kernel(
    part_ref, species_ref, count_ref, coupling_ref, coulomb_ref, rho_ref, ham_ref,
    around, parts, total_ref, cpad, send_sems, recv_sems,
):
    bands = lax.axis_size("band")
    me = lax.axis_index("band")
    slots = rho_ref.shape[0]
    up_x, down_x = {"dx": shifted("dx", 1)}, {"dx": shifted("dx", -1)}
    up_y, down_y = {"dyz": shifted("dyz", 1)}, {"dyz": shifted("dyz", -1)}
    up_xy = {"dx": shifted("dx", 1), "dyz": shifted("dyz", 1)}
    down_xy = {"dx": shifted("dx", -1), "dyz": shifted("dyz", -1)}
    others = [{"band": shifted("band", t)} for t in range(1, bands)]
    enter([up_x, down_x, up_y, down_y, up_xy, down_xy] + others)

    def remote(src, dst, sem, device):
        copy = pltpu.make_async_remote_copy(
            src_ref=src, dst_ref=dst, send_sem=send_sems.at[sem], recv_sem=recv_sems.at[sem],
            device_id=device, device_id_type=MESH,
        )
        copy.start()
        return copy

    copies = [
        remote(part_ref.at[c + 1], around.at[c], c, device)
        for c, device in enumerate((down_x, down_y, down_xy))
    ]
    eye = iota((slots, slots), 0) == iota((slots, slots), 1)
    kind = jnp.sum(jnp.where(eye, species_ref[...], 0), axis=1, keepdims=True)
    live = iota((slots, 1), 0) < count_ref[0]
    cpad[...] = jnp.zeros_like(cpad)
    comps = coupling_ref.shape[0]
    rho_high, rho_low = split(rho_ref[...])
    coul = jnp.zeros(rho_ref.shape, jnp.float32)
    for s in range(2):
        cpad[s, 0:comps, :] = coupling_ref[:, s, :]
        c_high, c_low = split(coulomb_ref[s])
        term = mm(rho_high, c_high) + (mm(rho_high, c_low) + mm(rho_low, c_high))
        coul = jnp.where(kind == s, 2.0 * term, coul)
    for copy in copies:
        copy.wait()
    mine = (part_ref[0] + around[0]) + (around[1] + around[2])
    total_ref[...] = mine
    parts[me] = mine
    copies = [
        remote(total_ref, parts.at[me], 2 + t, others[t - 1]) for t in range(1, bands)
    ]
    for copy in copies:
        copy.wait()
    moments = (parts[0] + parts[1]) + (parts[2] + parts[3])
    for b in range(4, bands):
        moments = moments + parts[b]
    rows = [pltpu.roll(moments, (128 - r * LANES) % 128, 1) for r in range(slots // GROUP)]
    moments = jnp.concatenate(rows, 0)[:, 0:LANES]
    summed = jnp.zeros(rho_ref.shape, jnp.float32)
    for s in range(2):
        term = jnp.dot(moments, cpad[s], precision=PRECISE, preferred_element_type=jnp.float32)
        summed = jnp.where(kind == s, term, summed)
    ham_ref[...] = jnp.where(live, summed + coul, 0.0)


def apply_kernel(ham_ref, proj_ref, out_ham_ref, out_hbm, out_ref, sems):
    out_ham_ref[...] = ham_ref[...]
    stores = []
    square = NI * NI
    row, col = iota((square, square), 0), iota((square, square), 1)
    spread = (lax.rem(row, NI) == lax.rem(col, NI)).astype(jnp.bfloat16)
    same_i = lax.rem(row, NI) == col // NI
    same_a = row // NI == col // NI
    for t in range(ham_ref.shape[0] // NI):
        block = ham_ref[t * NI : (t + 1) * NI, :]
        tall = jnp.broadcast_to(block[:, None, :], (NI, NI, square)).reshape(square, square)
        high, low = split(jnp.where(same_i, tall, 0.0))
        d_high = jnp.where(same_a, mm(high, spread), 0.0).astype(jnp.bfloat16)
        d_low = jnp.where(same_a, mm(low, spread), 0.0).astype(jnp.bfloat16)
        p_high, p_low = split(proj_ref[t * square : (t + 1) * square, :])
        out_ref[t * square : (t + 1) * square, :] = mm(d_high, p_high) + (
            mm(d_high, p_low) + mm(d_low, p_high)
        )
        rows = pl.ds(t * square, square)
        stores.append(pltpu.make_async_copy(out_ref.at[rows], out_hbm.at[rows], sems.at[t]))
        stores[-1].start()
    for store in stores:
        store.wait()


def local(
    density, hartree, box_root, species, atom_count, shape_functions, coupling, coulomb, rho_ij, projections
):
    f32 = jnp.float32
    wx, wy, depth = density.shape
    bands = lax.axis_size("band")
    slots = box_root.shape[1]
    kinds, comps, cells = shape_functions.shape
    vmem = pl.BlockSpec(memory_space=pltpu.VMEM)
    hbm = pl.BlockSpec(memory_space=pltpu.HBM)
    smem = pl.BlockSpec(memory_space=pltpu.SMEM)
    species_row = species.reshape(1, slots)

    face = lambda *s: pltpu.VMEM(s, f32)
    turned_shape = jax.ShapeDtypeStruct((kinds, comps * BOX, BOX * BOX), jnp.bfloat16)
    potential, atoms, high, low = pl.pallas_call(
        grid_kernel,
        name="grid_kernel",
        out_shape=(
            jax.ShapeDtypeStruct((wx, wy, depth), f32),
            jax.ShapeDtypeStruct((2, 8, 256), jnp.int32),
            turned_shape,
            turned_shape,
        ),
        in_specs=[hbm, hbm, hbm, vmem, vmem, smem],
        out_specs=(vmem,) * 4,
        scratch_shapes=[
            face(wx, wy, depth), face(wx, wy, depth), face(kinds, comps, cells),
            face(BOX * BOX, 128), pltpu.SemaphoreType.DMA((4,)),
            face(wx + 2, wy + 16, depth), face(wx + 2, wy, depth), face(wx, wy + 16, depth),
            face(wx, wy, depth), face(wx, wy, depth),
            face(2, wy, depth), face(2, wx, depth), face(wy, depth),
            face(2, wy, depth), face(2, wx, depth), face(2, wy, depth),
            face(2, wy, depth), face(2, wx, depth), face(wy, depth),
            face(2, wy, depth), face(2, wx, depth), face(2, wy, depth),
            pltpu.VMEM((8, 128), jnp.int32), pltpu.VMEM((3, 8, 128), jnp.int32),
            pltpu.SemaphoreType.DMA((15,)), pltpu.SemaphoreType.DMA((15,)),
        ],
        compiler_params=pltpu.CompilerParams(
            collective_id=0, has_side_effects=True, vmem_limit_bytes=56 * 1024 * 1024
        ),
    )(density, hartree, shape_functions.transpose(1, 0, 2), box_root, species_row, atom_count)

    lanes = GROUP * BOX
    potential, partial = pl.pallas_call(
        functools.partial(moment_kernel, depth * bands),
        name="moment_kernel",
        out_shape=(
            jax.ShapeDtypeStruct((wx, wy, depth), f32),
            jax.ShapeDtypeStruct((4, GROUP, 128), f32),
        ),
        in_specs=[smem, vmem, vmem, vmem],
        out_specs=(hbm, vmem),
        scratch_shapes=[
            face((wx + 2 * PAD) * (wy + 2 * PAD), depth),
            face(BOX * BOX, lanes), face(128, lanes), face(8 + 4 * slots, 128),
            pltpu.SemaphoreType.DMA,
        ],
        compiler_params=pltpu.CompilerParams(vmem_limit_bytes=VMEM_LIMIT),
    )(atoms, potential, high, low)

    ham = pl.pallas_call(
        block_kernel,
        name="block_kernel",
        out_shape=jax.ShapeDtypeStruct(rho_ij.shape, f32),
        in_specs=[vmem, vmem, smem, vmem, vmem, vmem],
        out_specs=vmem,
        scratch_shapes=[
            face(3, GROUP, 128), face(bands, GROUP, 128), face(GROUP, 128), face(2, LANES, NI * NI),
            pltpu.SemaphoreType.DMA((2 + bands,)), pltpu.SemaphoreType.DMA((2 + bands,)),
        ],
        compiler_params=pltpu.CompilerParams(
            collective_id=1, has_side_effects=True, vmem_limit_bytes=VMEM_LIMIT
        ),
    )(partial, species_row, atom_count, coupling.transpose(1, 0, 2), coulomb, rho_ij)

    width = projections.shape[2]
    ham, applied = pl.pallas_call(
        apply_kernel,
        name="apply_kernel",
        out_shape=(
            jax.ShapeDtypeStruct(rho_ij.shape, f32),
            jax.ShapeDtypeStruct((slots * NI, width), f32),
        ),
        in_specs=[vmem, vmem],
        out_specs=(vmem, hbm),
        scratch_shapes=[face(slots * NI, width), pltpu.SemaphoreType.DMA((slots // NI,))],
        compiler_params=pltpu.CompilerParams(vmem_limit_bytes=VMEM_LIMIT),
    )(ham, projections.reshape(slots * NI, width))
    return potential, ham, applied.reshape(slots, NI, width)


def solution(mesh):
    in_specs = (
        P("dx", "dyz", "band"),
        P("dx", "dyz", "band"),
        P(None, ("dx", "dyz")),
        P(("dx", "dyz")),
        P(("dx", "dyz")),
        P(),
        P(),
        P(),
        P(("dx", "dyz"), None),
        P(("dx", "dyz"), None, "band"),
    )
    out_specs = (P("dx", "dyz", "band"), P(("dx", "dyz"), None), P(("dx", "dyz"), None, "band"))
    return jax.shard_map(local, mesh=mesh, in_specs=in_specs, out_specs=out_specs, check_vma=False)
```

```python
import functools
import math

import jax
import jax.numpy as jnp
from jax import lax
from jax.experimental import pallas as pl
from jax.experimental.pallas import tpu as pltpu
from jax.sharding import PartitionSpec as P

BOX = 16
NI = 16
GROUP = 16
LANES = 32
PAD = 16
GRID_H = 0.15
KAPPA = 0.804
MU_COEF = 0.2195149727645171
PRECISE = lax.Precision.HIGHEST
HALF = 0.5 / GRID_H
PREF = -0.75 * (3.0 / math.pi) ** (1.0 / 3.0)
RED = 4.0 * (3.0 * math.pi**2) ** (2.0 / 3.0)
MESH = pl.DeviceIdType.MESH
VMEM_LIMIT = 56 * 1024 * 1024


def iota(shape, dim):
    return lax.broadcasted_iota(jnp.int32, shape, dim)


def shifted(axis, step):
    size = lax.axis_size(axis)
    return lax.rem(lax.axis_index(axis) + (step + size), size)


def enter(devices):
    barrier = pltpu.get_barrier_semaphore()
    for device in devices:
        pl.semaphore_signal(barrier, inc=1, device_id=device, device_id_type=MESH)
    pl.semaphore_wait(barrier, len(devices))


def split(value):
    high = value.astype(jnp.bfloat16)
    return high, (value - high.astype(jnp.float32)).astype(jnp.bfloat16)


def mm(a, b):
    return jnp.dot(a, b, preferred_element_type=jnp.float32)


def pack_ends(ref):
    wx, wy, depth = ref.shape
    lane = iota((wy, depth), 1)
    packed = jnp.zeros((wy, depth), jnp.float32)
    for x in range(wx):
        moved = pltpu.roll(ref[x], 2 * x + 1, 1)
        packed = jnp.where((lane == 2 * x) | (lane == 2 * x + 1), moved, packed)
    return packed


def join_ends(before, after):
    lane = iota(before.shape, 1)
    depth = before.shape[1]
    return jnp.where(
        lax.rem(lane, 2) == 1, pltpu.roll(before, 1, 1), pltpu.roll(after, depth - 1, 1)
    )


def turn_shapes(shape_ref, turned, high_ref, low_ref, s):
    comps, cells = shape_ref.shape[1:]
    lane, sub = iota((8, 128), 1) // BOX, iota((8, 128), 0)
    wraps = [(lane // bit) % 2 == 1 for bit in (1, 2, 4)]
    octets = (comps + 7) // 8
    row, col = iota((cells // BOX, cells // BOX), 0), iota((cells // BOX, cells // BOX), 1)
    order = (row // 8 == col // 8) & (lax.rem(row + col, 8) == 0)
    order = order.astype(jnp.bfloat16)
    for o in range(octets):
        for t in range(cells // 128):
            here = slice(t * 128, (t + 1) * 128)
            if 8 * o + 8 <= comps:
                tile = shape_ref[s, 8 * o : 8 * o + 8, here]
            else:
                tile = jnp.broadcast_to(shape_ref[s, 8 * o : 8 * o + 1, here], (8, 128))
            tile = pltpu.roll(tile, 0, 1, stride=BOX, stride_axis=0)
            for bit, wrap in zip((1, 2, 4), wraps):
                tile = jnp.where(wrap, pltpu.roll(tile, 8 - bit, 0), tile)
            tile = pltpu.roll(tile, 0, 1, stride=BOX, stride_axis=0)
            turned[t * 8 : (t + 1) * 8, :] = tile
        block = turned[...].T
        rows = min(128, (comps - 8 * o) * BOX)
        high, low = split(block[0:rows, :])
        high_ref[s, o * 128 : o * 128 + rows, :] = mm(high, order).astype(jnp.bfloat16)
        low_ref[s, o * 128 : o * 128 + rows, :] = mm(low, order).astype(jnp.bfloat16)


def grid_kernel(
    dens_hbm, hart_hbm, shape_hbm, root_ref, species_ref, count_ref,
    pot_ref, list_ref, high_ref, low_ref,
    dens_ref, hart_ref, shape_ref, turned, local_sems,
    dpad, fxp, fyp, fz, slope_n_ref,
    send_x, send_y, send_z, recv_x, recv_y, recv_z,
    gsend_x, gsend_y, gsend_z, grecv_x, grecv_y, grecv_z,
    plan_send, plan_recv, send_sems, recv_sems,
):
    wx, wy, depth = dens_ref.shape
    loads = [
        pltpu.make_async_copy(src, dst, local_sems.at[i])
        for i, (src, dst) in enumerate(
            (
                (dens_hbm, dens_ref),
                (shape_hbm.at[:, 0, :], shape_ref.at[0]),
                (shape_hbm.at[:, 1, :], shape_ref.at[1]),
                (hart_hbm, hart_ref),
            )
        )
    ]
    for load in loads:
        load.start()
    up_x, down_x = {"dx": shifted("dx", 1)}, {"dx": shifted("dx", -1)}
    up_y, down_y = {"dyz": shifted("dyz", 1)}, {"dyz": shifted("dyz", -1)}
    up_z, down_z = {"band": shifted("band", 1)}, {"band": shifted("band", -1)}
    up_xy = {"dx": shifted("dx", 1), "dyz": shifted("dyz", 1)}
    down_xy = {"dx": shifted("dx", -1), "dyz": shifted("dyz", -1)}
    slots = root_ref.shape[1]

    def remote(src, dst, sem, device):
        copy = pltpu.make_async_remote_copy(
            src_ref=src, dst_ref=dst, send_sem=send_sems.at[sem], recv_sem=recv_sems.at[sem],
            device_id=device, device_id_type=MESH,
        )
        copy.start()
        return copy

    loads[0].wait()
    send_x[0] = dens_ref[wx - 1]
    send_x[1] = dens_ref[0]
    send_y[0] = dens_ref[:, wy - 1, :]
    send_y[1] = dens_ref[:, 0, :]
    send_z[...] = pack_ends(dens_ref)
    plan_send[...] = jnp.zeros_like(plan_send)
    plan_send[0:1, 0:slots] = root_ref[0:1, :] - lax.axis_index("dx") * wx
    plan_send[1:2, 0:slots] = root_ref[1:2, :] - lax.axis_index("dyz") * wy
    plan_send[2:3, 0:slots] = root_ref[2:3, :]
    plan_send[3:4, 0:slots] = species_ref[...]
    plan_send[4:5, :] = jnp.full((1, 128), count_ref[0], jnp.int32)

    enter([up_x, down_x, up_y, down_y, up_z, down_z, up_xy, down_xy])
    first = [
        remote(send_z, recv_z.at[0], 0, up_z),
        remote(send_z, recv_z.at[1], 1, down_z),
        remote(send_y.at[0], recv_y.at[0], 2, up_y),
        remote(send_y.at[1], recv_y.at[1], 3, down_y),
        remote(send_x.at[0], recv_x.at[0], 4, up_x),
        remote(send_x.at[1], recv_x.at[1], 5, down_x),
    ]
    plans = [
        remote(plan_send, plan_recv.at[0], 6, up_x),
        remote(plan_send, plan_recv.at[1], 7, up_y),
        remote(plan_send, plan_recv.at[2], 8, up_xy),
    ]
    dpad[1 : wx + 1, 8 : wy + 8, :] = dens_ref[...]
    loads[1].wait()
    turn_shapes(shape_ref, turned, high_ref, low_ref, 0)
    for copy in first:
        copy.wait()
    dpad[0, 8 : wy + 8, :] = recv_x[0]
    dpad[wx + 1, 8 : wy + 8, :] = recv_x[1]
    dpad[1 : wx + 1, 7, :] = recv_y[0]
    dpad[1 : wx + 1, wy + 8, :] = recv_y[1]
    ends = join_ends(recv_z[0], recv_z[1])
    lane = iota((wy, depth), 1)

    def flux_step(x):
        here = dpad[x + 1, 8 : wy + 8, :]
        gx = (dpad[x + 2, 8 : wy + 8, :] - dpad[x, 8 : wy + 8, :]) * HALF
        gy = (dpad[x + 1, 9 : wy + 9, :] - dpad[x + 1, 7 : wy + 7, :]) * HALF
        end = pltpu.roll(ends, depth - 1 - 2 * x, 1)
        after = jnp.where(lane == depth - 1, end, pltpu.roll(here, depth - 1, 1))
        before = jnp.where(lane == 0, end, pltpu.roll(here, 1, 1))
        gz = (after - before) * HALF
        sigma = gx * gx + gy * gy + gz * gz
        log_n = jnp.log(here)
        cube = jnp.exp(log_n * (1.0 / 3.0))
        power = here * cube
        scaled = RED * power * power
        summed = scaled + (MU_COEF / KAPPA) * sigma
        both = 1.0 / (power * summed)
        u = scaled * power * both
        slope_s = (PREF / RED * MU_COEF) * u * u * (summed * both)
        slope_n_ref[x] = (4.0 / 3.0 * PREF) * cube * (1.0 + KAPPA - KAPPA * u * (3.0 - 2.0 * u))
        fxp[x + 1] = slope_s * gx
        fyp[x, 8 : wy + 8, :] = slope_s * gy
        fz[x] = slope_s * gz

    per = 4

    def flux_steps(t, carry):
        for k in range(per):
            flux_step(t * per + k)
        return carry

    lax.fori_loop(0, wx // per, flux_steps, 0)

    gsend_x[0] = fxp[wx]
    gsend_x[1] = fxp[1]
    gsend_y[0] = fyp[:, wy + 7, :]
    gsend_y[1] = fyp[:, 8, :]
    gsend_z[...] = pack_ends(fz)
    second = [
        remote(gsend_z, grecv_z.at[0], 9, up_z),
        remote(gsend_z, grecv_z.at[1], 10, down_z),
        remote(gsend_y.at[0], grecv_y.at[0], 11, up_y),
        remote(gsend_y.at[1], grecv_y.at[1], 12, down_y),
        remote(gsend_x.at[0], grecv_x.at[0], 13, up_x),
        remote(gsend_x.at[1], grecv_x.at[1], 14, down_x),
    ]

    for copy in plans:
        copy.wait()
    depth_all = depth * lax.axis_size("band")
    first_z = lax.axis_index("band") * depth
    columns = []
    for c in range(4):
        plan = plan_send[...] if c == 0 else plan_recv[c - 1]
        x = plan[0:1, :] - (wx if c in (1, 3) else 0)
        y = plan[1:2, :] - (wy if c in (2, 3) else 0)
        z = plan[2:3, :] - first_z
        z = jnp.where(z < 0, z + depth_all, z)
        slot = iota((1, 128), 1)
        meets = (slot < plan[4:5, :]) & (slot < slots)
        meets &= (x > -BOX) & (y > -BOX) & (x < wx) & (y < wy)
        meets &= (z < depth) | (z > depth_all - BOX)
        rows = (x + PAD) * (wy + 2 * PAD) + (y + PAD)
        dest = 8 + c * slots + slot
        columns.append([v.astype(jnp.int32) for v in (meets, rows, z, dest, plan[3:4, :])])
    left = iota((1, 128), 1) < slots
    merged = []
    for f in range(5):
        halves = [
            jnp.where(left, columns[c][f], pltpu.roll(columns[c + 1][f], slots, 1)) for c in (0, 2)
        ]
        merged.append(jnp.concatenate(halves, 1))
    meets, rows, z, dest, kind = merged
    wide = 256
    upper = (iota((wide, wide), 0) <= iota((wide, wide), 1)).astype(jnp.bfloat16)
    row8 = iota((8, wide), 0)
    picked = jnp.where((meets == 1) & (kind == row8), 1.0, 0.0)
    order = mm(picked.astype(jnp.bfloat16), upper)
    place = iota((wide, wide), 0).astype(jnp.float32) + 1.0
    fields = jnp.where(row8 == 0, rows, jnp.where(row8 == 1, z, jnp.where(row8 == 2, dest, 0)))
    f_high, f_low = split(fields.astype(jnp.float32))
    across = (((1,), (1,)), ((), ()))
    for s in range(2):
        total = jnp.sum(picked[s : s + 1, :], axis=1, keepdims=True)
        spot = jnp.where(picked[s : s + 1, :] > 0.5, order[s : s + 1, :], 0.0)
        onehot = (spot == place).astype(jnp.bfloat16)
        got = lax.dot_general(f_high, onehot, across, preferred_element_type=jnp.float32)
        got = got + lax.dot_general(f_low, onehot, across, preferred_element_type=jnp.float32)
        got = jnp.where(row8 == 3, total, got)
        list_ref[s] = (got + 0.5).astype(jnp.int32)
    loads[2].wait()
    turn_shapes(shape_ref, turned, high_ref, low_ref, 1)

    loads[3].wait()
    for copy in second:
        copy.wait()
    fxp[0] = grecv_x[0]
    fxp[wx + 1] = grecv_x[1]
    fyp[:, 7, :] = grecv_y[0]
    fyp[:, wy + 8, :] = grecv_y[1]
    flux_ends = join_ends(grecv_z[0], grecv_z[1])

    def pot_step(x):
        here = fz[x]
        end = pltpu.roll(flux_ends, depth - 1 - 2 * x, 1)
        after = jnp.where(lane == depth - 1, end, pltpu.roll(here, depth - 1, 1))
        before = jnp.where(lane == 0, end, pltpu.roll(here, 1, 1))
        spread = (fxp[x + 2] - fxp[x]) * HALF
        spread = spread + (fyp[x, 9 : wy + 9, :] - fyp[x, 7 : wy + 7, :]) * HALF
        spread = spread + (after - before) * HALF
        pot_ref[x] = hart_ref[x] + slope_n_ref[x] - 2.0 * spread

    def pot_steps(t, carry):
        for k in range(per):
            pot_step(t * per + k)
        return carry

    lax.fori_loop(0, wx // per, pot_steps, 0)


def moment_kernel(
    depth_all, list_ref, pot_hbm, high_hbm, low_hbm, out_pot_ref, out_ref,
    pot_ref, high_ref, low_ref, padded, gathered, folded, sums, load_sems, sem,
):
    loads = [
        pltpu.make_async_copy(src, dst, load_sems.at[i])
        for i, (src, dst) in enumerate(
            ((pot_hbm, pot_ref), (high_hbm, high_ref), (low_hbm, low_ref))
        )
    ]
    for load in loads:
        load.start()
    wx, wy, depth = pot_ref.shape
    rows_y = wy + 2 * PAD
    comps = high_ref.shape[1] // BOX
    padded[...] = jnp.zeros_like(padded)
    sums[...] = jnp.zeros_like(sums)
    folded[...] = jnp.zeros_like(folded)
    loads[0].wait()
    store = pltpu.make_async_copy(pot_ref, out_pot_ref, sem)
    store.start()
    for x in range(wx):
        start = (x + PAD) * rows_y + PAD
        padded[start : start + wy, :] = pot_ref[x]
    loads[1].wait()
    loads[2].wait()
    lanes = GROUP * BOX
    per_tile = 128 // BOX
    lane = iota((BOX, 128), 1)
    adder = (iota((GROUP, lanes), 0) == iota((GROUP, lanes), 1) // BOX).astype(jnp.float32)
    keep = lax.rem(iota((BOX, lanes), 1), BOX) == iota((BOX, lanes), 0)

    for s in range(2):
        total = list_ref[s, 3, 0]

        def one_group(g, carry, s=s, total=total):
            for tile in range(lanes // 128):
                first = g * GROUP + tile * per_tile
                across = slice(tile * 128, (tile + 1) * 128)

                @pl.when(first < total)
                def _(first=first, across=across):
                    plan = []
                    for q in range(per_tile):
                        left = q * BOX
                        z = list_ref[s, 1, first + q]
                        shift = lax.rem(left + depth_all - z, depth)
                        cell = z + lane - left
                        cell = jnp.where(cell >= depth_all, cell - depth_all, cell)
                        mine = (lane >= left) & (lane < left + BOX) & (cell < depth)
                        plan.append((list_ref[s, 0, first + q], shift, mine))
                    for i in range(BOX):
                        made = jnp.zeros((BOX, 128), jnp.float32)
                        for row, shift, mine in plan:
                            piece = padded[pl.ds(row + i * rows_y, BOX), :]
                            made = jnp.where(mine, pltpu.roll(piece, shift, 1), made)
                        gathered[i * BOX : (i + 1) * BOX, across] = made

                @pl.when(first >= total)
                def _(across=across):
                    gathered[:, across] = jnp.zeros((BOX * BOX, 128), jnp.float32)

            g_high, g_low = split(gathered[...])
            product = mm(high_ref[s], g_high) + (mm(high_ref[s], g_low) + mm(low_ref[s], g_high))
            product = jnp.where(keep[None], product.reshape(comps, BOX, lanes), 0.0)
            folded[0:comps, :] = jnp.sum(product, axis=1)
            result = lax.dot_general(
                adder, folded[...], (((1,), (1,)), ((), ())), precision=PRECISE,
                preferred_element_type=jnp.float32,
            ) * (GRID_H**3)
            for q in range(GROUP):
                spot = list_ref[s, 2, g * GROUP + q]
                sums[pl.ds(spot, 1), :] = result[q : q + 1, :]
            return carry

        lax.fori_loop(0, (total + GROUP - 1) // GROUP, one_group, 0)
    slots = (sums.shape[0] - 8) // 4
    for c in range(4):
        held = jnp.zeros(out_ref.shape[1:], jnp.float32)
        for r in range(slots // GROUP):
            start = 8 + c * slots + r * GROUP
            held = held + pltpu.roll(sums[start : start + GROUP, :], r * LANES, 1)
        out_ref[c] = held
    store.wait()


def block_kernel(
    part_ref, species_ref, count_ref, coupling_ref, coulomb_hbm, rho_hbm, ham_ref,
    coulomb_ref, rho_ref, load_sems, around, parts, total_ref, cpad, send_sems, recv_sems,
):
    bands = lax.axis_size("band")
    me = lax.axis_index("band")
    slots = rho_ref.shape[0]
    up_x, down_x = {"dx": shifted("dx", 1)}, {"dx": shifted("dx", -1)}
    up_y, down_y = {"dyz": shifted("dyz", 1)}, {"dyz": shifted("dyz", -1)}
    up_xy = {"dx": shifted("dx", 1), "dyz": shifted("dyz", 1)}
    down_xy = {"dx": shifted("dx", -1), "dyz": shifted("dyz", -1)}
    others = [{"band": shifted("band", t)} for t in range(1, bands)]
    loads = [
        pltpu.make_async_copy(coulomb_hbm, coulomb_ref, load_sems.at[0]),
        pltpu.make_async_copy(rho_hbm, rho_ref, load_sems.at[1]),
    ]
    for load in loads:
        load.start()
    enter([up_x, down_x, up_y, down_y, up_xy, down_xy] + others)

    def remote(src, dst, sem, device):
        copy = pltpu.make_async_remote_copy(
            src_ref=src, dst_ref=dst, send_sem=send_sems.at[sem], recv_sem=recv_sems.at[sem],
            device_id=device, device_id_type=MESH,
        )
        copy.start()
        return copy

    copies = [
        remote(part_ref.at[c + 1], around.at[c], c, device)
        for c, device in enumerate((down_x, down_y, down_xy))
    ]
    eye = iota((slots, slots), 0) == iota((slots, slots), 1)
    kind = jnp.sum(jnp.where(eye, species_ref[...], 0), axis=1, keepdims=True)
    live = iota((slots, 1), 0) < count_ref[0]
    cpad[...] = jnp.zeros_like(cpad)
    comps = coupling_ref.shape[0]
    for load in loads:
        load.wait()
    rho_high, rho_low = split(rho_ref[...])
    coul = jnp.zeros(rho_ref.shape, jnp.float32)
    for s in range(2):
        cpad[s, 0:comps, :] = coupling_ref[:, s, :]
        c_high, c_low = split(coulomb_ref[s])
        term = mm(rho_high, c_high) + (mm(rho_high, c_low) + mm(rho_low, c_high))
        coul = jnp.where(kind == s, 2.0 * term, coul)
    for copy in copies:
        copy.wait()
    mine = (part_ref[0] + around[0]) + (around[1] + around[2])
    total_ref[...] = mine
    parts[me] = mine
    copies = [
        remote(total_ref, parts.at[me], 2 + t, others[t - 1]) for t in range(1, bands)
    ]
    for copy in copies:
        copy.wait()
    moments = (parts[0] + parts[1]) + (parts[2] + parts[3])
    for b in range(4, bands):
        moments = moments + parts[b]
    rows = [pltpu.roll(moments, (128 - r * LANES) % 128, 1) for r in range(slots // GROUP)]
    moments = jnp.concatenate(rows, 0)[:, 0:LANES]
    summed = jnp.zeros(rho_ref.shape, jnp.float32)
    for s in range(2):
        term = jnp.dot(moments, cpad[s], precision=PRECISE, preferred_element_type=jnp.float32)
        summed = jnp.where(kind == s, term, summed)
    ham_ref[...] = jnp.where(live, summed + coul, 0.0)


def apply_kernel(ham_ref, proj_hbm, out_ham_ref, out_hbm, proj_ref, out_ref, load_sems, sems):
    loads = []
    for t in range(ham_ref.shape[0] // NI):
        rows = pl.ds(t * NI * NI, NI * NI)
        loads.append(pltpu.make_async_copy(proj_hbm.at[rows], proj_ref.at[rows], load_sems.at[t]))
        loads[-1].start()
    out_ham_ref[...] = ham_ref[...]
    stores = []
    square = NI * NI
    row, col = iota((square, square), 0), iota((square, square), 1)
    spread = (lax.rem(row, NI) == lax.rem(col, NI)).astype(jnp.bfloat16)
    same_i = lax.rem(row, NI) == col // NI
    same_a = row // NI == col // NI
    for t in range(ham_ref.shape[0] // NI):
        block = ham_ref[t * NI : (t + 1) * NI, :]
        tall = jnp.broadcast_to(block[:, None, :], (NI, NI, square)).reshape(square, square)
        high, low = split(jnp.where(same_i, tall, 0.0))
        d_high = jnp.where(same_a, mm(high, spread), 0.0).astype(jnp.bfloat16)
        d_low = jnp.where(same_a, mm(low, spread), 0.0).astype(jnp.bfloat16)
        loads[t].wait()
        p_high, p_low = split(proj_ref[t * square : (t + 1) * square, :])
        out_ref[t * square : (t + 1) * square, :] = mm(d_high, p_high) + (
            mm(d_high, p_low) + mm(d_low, p_high)
        )
        rows = pl.ds(t * square, square)
        stores.append(pltpu.make_async_copy(out_ref.at[rows], out_hbm.at[rows], sems.at[t]))
        stores[-1].start()
    for store in stores:
        store.wait()


def local(
    density, hartree, box_root, species, atom_count, shape_functions, coupling, coulomb, rho_ij, projections
):
    f32 = jnp.float32
    wx, wy, depth = density.shape
    bands = lax.axis_size("band")
    slots = box_root.shape[1]
    kinds, comps, cells = shape_functions.shape
    vmem = pl.BlockSpec(memory_space=pltpu.VMEM)
    hbm = pl.BlockSpec(memory_space=pltpu.HBM)
    smem = pl.BlockSpec(memory_space=pltpu.SMEM)
    species_row = species.reshape(1, slots)

    face = lambda *s: pltpu.VMEM(s, f32)
    turned_shape = jax.ShapeDtypeStruct((kinds, comps * BOX, BOX * BOX), jnp.bfloat16)
    potential, atoms, high, low = pl.pallas_call(
        grid_kernel,
        name="grid_kernel",
        out_shape=(
            jax.ShapeDtypeStruct((wx, wy, depth), f32),
            jax.ShapeDtypeStruct((2, 8, 256), jnp.int32),
            turned_shape,
            turned_shape,
        ),
        in_specs=[hbm, hbm, hbm, vmem, vmem, smem],
        out_specs=(vmem,) * 4,
        scratch_shapes=[
            face(wx, wy, depth), face(wx, wy, depth), face(kinds, comps, cells),
            face(BOX * BOX, 128), pltpu.SemaphoreType.DMA((4,)),
            face(wx + 2, wy + 16, depth), face(wx + 2, wy, depth), face(wx, wy + 16, depth),
            face(wx, wy, depth), face(wx, wy, depth),
            face(2, wy, depth), face(2, wx, depth), face(wy, depth),
            face(2, wy, depth), face(2, wx, depth), face(2, wy, depth),
            face(2, wy, depth), face(2, wx, depth), face(wy, depth),
            face(2, wy, depth), face(2, wx, depth), face(2, wy, depth),
            pltpu.VMEM((8, 128), jnp.int32), pltpu.VMEM((3, 8, 128), jnp.int32),
            pltpu.SemaphoreType.DMA((15,)), pltpu.SemaphoreType.DMA((15,)),
        ],
        compiler_params=pltpu.CompilerParams(
            collective_id=0, has_side_effects=True, vmem_limit_bytes=56 * 1024 * 1024
        ),
    )(density, hartree, shape_functions.transpose(1, 0, 2), box_root, species_row, atom_count)

    lanes = GROUP * BOX
    potential, partial = pl.pallas_call(
        functools.partial(moment_kernel, depth * bands),
        name="moment_kernel",
        out_shape=(
            jax.ShapeDtypeStruct((wx, wy, depth), f32),
            jax.ShapeDtypeStruct((4, GROUP, 128), f32),
        ),
        in_specs=[smem, hbm, hbm, hbm],
        out_specs=(hbm, vmem),
        scratch_shapes=[
            face(wx, wy, depth),
            pltpu.VMEM(turned_shape.shape, jnp.bfloat16), pltpu.VMEM(turned_shape.shape, jnp.bfloat16),
            face((wx + 2 * PAD) * (wy + 2 * PAD), depth),
            face(BOX * BOX, lanes), face(128, lanes), face(8 + 4 * slots, 128),
            pltpu.SemaphoreType.DMA((3,)), pltpu.SemaphoreType.DMA,
        ],
        compiler_params=pltpu.CompilerParams(vmem_limit_bytes=VMEM_LIMIT),
    )(atoms, potential, high, low)

    ham = pl.pallas_call(
        block_kernel,
        name="block_kernel",
        out_shape=jax.ShapeDtypeStruct(rho_ij.shape, f32),
        in_specs=[vmem, vmem, smem, vmem, hbm, hbm],
        out_specs=vmem,
        scratch_shapes=[
            face(*coulomb.shape), face(*rho_ij.shape), pltpu.SemaphoreType.DMA((2,)),
            face(3, GROUP, 128), face(bands, GROUP, 128), face(GROUP, 128), face(2, LANES, NI * NI),
            pltpu.SemaphoreType.DMA((2 + bands,)), pltpu.SemaphoreType.DMA((2 + bands,)),
        ],
        compiler_params=pltpu.CompilerParams(
            collective_id=1, has_side_effects=True, vmem_limit_bytes=VMEM_LIMIT
        ),
    )(partial, species_row, atom_count, coupling.transpose(1, 0, 2), coulomb, rho_ij)

    width = projections.shape[2]
    ham, applied = pl.pallas_call(
        apply_kernel,
        name="apply_kernel",
        out_shape=(
            jax.ShapeDtypeStruct(rho_ij.shape, f32),
            jax.ShapeDtypeStruct((slots * NI, width), f32),
        ),
        in_specs=[vmem, hbm],
        out_specs=(vmem, hbm),
        scratch_shapes=[
            face(slots * NI, width), face(slots * NI, width),
            pltpu.SemaphoreType.DMA((slots // NI,)), pltpu.SemaphoreType.DMA((slots // NI,)),
        ],
        compiler_params=pltpu.CompilerParams(vmem_limit_bytes=VMEM_LIMIT),
    )(ham, projections.reshape(slots * NI, width))
    return potential, ham, applied.reshape(slots, NI, width)


def solution(mesh):
    in_specs = (
        P("dx", "dyz", "band"),
        P("dx", "dyz", "band"),
        P(None, ("dx", "dyz")),
        P(("dx", "dyz")),
        P(("dx", "dyz")),
        P(),
        P(),
        P(),
        P(("dx", "dyz"), None),
        P(("dx", "dyz"), None, "band"),
    )
    out_specs = (P("dx", "dyz", "band"), P(("dx", "dyz"), None), P(("dx", "dyz"), None, "band"))
    return jax.shard_map(local, mesh=mesh, in_specs=in_specs, out_specs=out_specs, check_vma=False)
```

```python
import functools
import math

import jax
import jax.numpy as jnp
from jax import lax
from jax.experimental import pallas as pl
from jax.experimental.pallas import tpu as pltpu
from jax.sharding import PartitionSpec as P

BOX = 16
NI = 16
GROUP = 16
LANES = 32
PAD = 16
GRID_H = 0.15
KAPPA = 0.804
MU_COEF = 0.2195149727645171
PRECISE = lax.Precision.HIGHEST
HALF = 0.5 / GRID_H
PREF = -0.75 * (3.0 / math.pi) ** (1.0 / 3.0)
RED = 4.0 * (3.0 * math.pi**2) ** (2.0 / 3.0)
MESH = pl.DeviceIdType.MESH
VMEM_LIMIT = 56 * 1024 * 1024


def iota(shape, dim):
    return lax.broadcasted_iota(jnp.int32, shape, dim)


def shifted(axis, step):
    size = lax.axis_size(axis)
    return lax.rem(lax.axis_index(axis) + (step + size), size)


def enter(devices):
    barrier = pltpu.get_barrier_semaphore()
    for device in devices:
        pl.semaphore_signal(barrier, inc=1, device_id=device, device_id_type=MESH)
    pl.semaphore_wait(barrier, len(devices))


def split(value):
    high = value.astype(jnp.bfloat16)
    return high, (value - high.astype(jnp.float32)).astype(jnp.bfloat16)


def mm(a, b):
    return jnp.dot(a, b, preferred_element_type=jnp.float32)


def pack_ends(ref):
    wx, wy, depth = ref.shape
    lane = iota((wy, depth), 1)
    packed = jnp.zeros((wy, depth), jnp.float32)
    for x in range(wx):
        moved = pltpu.roll(ref[x], 2 * x + 1, 1)
        packed = jnp.where((lane == 2 * x) | (lane == 2 * x + 1), moved, packed)
    return packed


def join_ends(before, after):
    lane = iota(before.shape, 1)
    depth = before.shape[1]
    return jnp.where(
        lax.rem(lane, 2) == 1, pltpu.roll(before, 1, 1), pltpu.roll(after, depth - 1, 1)
    )


def turn_shapes(shape_ref, turned, high_ref, low_ref, s):
    comps, cells = shape_ref.shape[1:]
    lane, sub = iota((8, 128), 1) // BOX, iota((8, 128), 0)
    wraps = [(lane // bit) % 2 == 1 for bit in (1, 2, 4)]
    octets = (comps + 7) // 8
    row, col = iota((cells // BOX, cells // BOX), 0), iota((cells // BOX, cells // BOX), 1)
    order = (row // 8 == col // 8) & (lax.rem(row + col, 8) == 0)
    order = order.astype(jnp.bfloat16)
    for o in range(octets):
        for t in range(cells // 128):
            here = slice(t * 128, (t + 1) * 128)
            if 8 * o + 8 <= comps:
                tile = shape_ref[s, 8 * o : 8 * o + 8, here]
            else:
                tile = jnp.broadcast_to(shape_ref[s, 8 * o : 8 * o + 1, here], (8, 128))
            tile = pltpu.roll(tile, 0, 1, stride=BOX, stride_axis=0)
            for bit, wrap in zip((1, 2, 4), wraps):
                tile = jnp.where(wrap, pltpu.roll(tile, 8 - bit, 0), tile)
            tile = pltpu.roll(tile, 0, 1, stride=BOX, stride_axis=0)
            turned[t * 8 : (t + 1) * 8, :] = tile
        block = turned[...].T
        rows = min(128, (comps - 8 * o) * BOX)
        high, low = split(block[0:rows, :])
        high_ref[s, o * 128 : o * 128 + rows, :] = mm(high, order).astype(jnp.bfloat16)
        low_ref[s, o * 128 : o * 128 + rows, :] = mm(low, order).astype(jnp.bfloat16)


def grid_kernel(
    dens_hbm, hart_hbm, shape_hbm, root_ref, species_ref, count_ref,
    pot_ref, list_ref, high_ref, low_ref,
    dens_ref, hart_ref, shape_ref, turned, local_sems,
    dpad, fxp, fyp, fz, slope_n_ref,
    send_x, send_y, send_z, recv_x, recv_y, recv_z,
    gsend_x, gsend_y, gsend_z, grecv_x, grecv_y, grecv_z,
    plan_send, plan_recv, send_sems, recv_sems,
):
    wx, wy, depth = dens_ref.shape
    loads = [
        pltpu.make_async_copy(src, dst, local_sems.at[i])
        for i, (src, dst) in enumerate(
            (
                (dens_hbm, dens_ref),
                (shape_hbm.at[:, 0, :], shape_ref.at[0]),
                (shape_hbm.at[:, 1, :], shape_ref.at[1]),
                (hart_hbm, hart_ref),
            )
        )
    ]
    for load in loads:
        load.start()
    up_x, down_x = {"dx": shifted("dx", 1)}, {"dx": shifted("dx", -1)}
    up_y, down_y = {"dyz": shifted("dyz", 1)}, {"dyz": shifted("dyz", -1)}
    up_z, down_z = {"band": shifted("band", 1)}, {"band": shifted("band", -1)}
    up_xy = {"dx": shifted("dx", 1), "dyz": shifted("dyz", 1)}
    down_xy = {"dx": shifted("dx", -1), "dyz": shifted("dyz", -1)}
    slots = root_ref.shape[1]

    def remote(src, dst, sem, device):
        copy = pltpu.make_async_remote_copy(
            src_ref=src, dst_ref=dst, send_sem=send_sems.at[sem], recv_sem=recv_sems.at[sem],
            device_id=device, device_id_type=MESH,
        )
        copy.start()
        return copy

    loads[0].wait()
    send_x[0] = dens_ref[wx - 1]
    send_x[1] = dens_ref[0]
    send_y[0] = dens_ref[:, wy - 1, :]
    send_y[1] = dens_ref[:, 0, :]
    send_z[...] = pack_ends(dens_ref)
    plan_send[...] = jnp.zeros_like(plan_send)
    plan_send[0:1, 0:slots] = root_ref[0:1, :] - lax.axis_index("dx") * wx
    plan_send[1:2, 0:slots] = root_ref[1:2, :] - lax.axis_index("dyz") * wy
    plan_send[2:3, 0:slots] = root_ref[2:3, :]
    plan_send[3:4, 0:slots] = species_ref[...]
    plan_send[4:5, :] = jnp.full((1, 128), count_ref[0], jnp.int32)

    enter([up_x, down_x, up_y, down_y, up_z, down_z, up_xy, down_xy])
    first = [
        remote(send_z, recv_z.at[0], 0, up_z),
        remote(send_z, recv_z.at[1], 1, down_z),
        remote(send_y.at[0], recv_y.at[0], 2, up_y),
        remote(send_y.at[1], recv_y.at[1], 3, down_y),
        remote(send_x.at[0], recv_x.at[0], 4, up_x),
        remote(send_x.at[1], recv_x.at[1], 5, down_x),
    ]
    plans = [
        remote(plan_send, plan_recv.at[0], 6, up_x),
        remote(plan_send, plan_recv.at[1], 7, up_y),
        remote(plan_send, plan_recv.at[2], 8, up_xy),
    ]
    dpad[1 : wx + 1, 8 : wy + 8, :] = dens_ref[...]
    loads[1].wait()
    turn_shapes(shape_ref, turned, high_ref, low_ref, 0)
    for copy in first:
        copy.wait()
    dpad[0, 8 : wy + 8, :] = recv_x[0]
    dpad[wx + 1, 8 : wy + 8, :] = recv_x[1]
    dpad[1 : wx + 1, 7, :] = recv_y[0]
    dpad[1 : wx + 1, wy + 8, :] = recv_y[1]
    ends = join_ends(recv_z[0], recv_z[1])
    lane = iota((wy, depth), 1)

    def flux_step(x):
        here = dpad[x + 1, 8 : wy + 8, :]
        gx = (dpad[x + 2, 8 : wy + 8, :] - dpad[x, 8 : wy + 8, :]) * HALF
        gy = (dpad[x + 1, 9 : wy + 9, :] - dpad[x + 1, 7 : wy + 7, :]) * HALF
        end = pltpu.roll(ends, depth - 1 - 2 * x, 1)
        after = jnp.where(lane == depth - 1, end, pltpu.roll(here, depth - 1, 1))
        before = jnp.where(lane == 0, end, pltpu.roll(here, 1, 1))
        gz = (after - before) * HALF
        sigma = gx * gx + gy * gy + gz * gz
        log_n = jnp.log(here)
        cube = jnp.exp(log_n * (1.0 / 3.0))
        power = here * cube
        scaled = RED * power * power
        summed = scaled + (MU_COEF / KAPPA) * sigma
        both = 1.0 / (power * summed)
        u = scaled * power * both
        slope_s = (PREF / RED * MU_COEF) * u * u * (summed * both)
        slope_n_ref[x] = (4.0 / 3.0 * PREF) * cube * (1.0 + KAPPA - KAPPA * u * (3.0 - 2.0 * u))
        fxp[x + 1] = slope_s * gx
        fyp[x, 8 : wy + 8, :] = slope_s * gy
        fz[x] = slope_s * gz

    per = 4

    def flux_steps(t, carry):
        for k in range(per):
            flux_step(t * per + k)
        return carry

    lax.fori_loop(0, wx // per, flux_steps, 0)

    gsend_x[0] = fxp[wx]
    gsend_x[1] = fxp[1]
    gsend_y[0] = fyp[:, wy + 7, :]
    gsend_y[1] = fyp[:, 8, :]
    gsend_z[...] = pack_ends(fz)
    second = [
        remote(gsend_z, grecv_z.at[0], 9, up_z),
        remote(gsend_z, grecv_z.at[1], 10, down_z),
        remote(gsend_y.at[0], grecv_y.at[0], 11, up_y),
        remote(gsend_y.at[1], grecv_y.at[1], 12, down_y),
        remote(gsend_x.at[0], grecv_x.at[0], 13, up_x),
        remote(gsend_x.at[1], grecv_x.at[1], 14, down_x),
    ]

    for copy in plans:
        copy.wait()
    depth_all = depth * lax.axis_size("band")
    first_z = lax.axis_index("band") * depth
    columns = []
    for c in range(4):
        plan = plan_send[...] if c == 0 else plan_recv[c - 1]
        x = plan[0:1, :] - (wx if c in (1, 3) else 0)
        y = plan[1:2, :] - (wy if c in (2, 3) else 0)
        z = plan[2:3, :] - first_z
        z = jnp.where(z < 0, z + depth_all, z)
        slot = iota((1, 128), 1)
        meets = (slot < plan[4:5, :]) & (slot < slots)
        meets &= (x > -BOX) & (y > -BOX) & (x < wx) & (y < wy)
        meets &= (z < depth) | (z > depth_all - BOX)
        rows = (x + PAD) * (wy + 2 * PAD) + (y + PAD)
        dest = 8 + c * slots + slot
        columns.append([v.astype(jnp.int32) for v in (meets, rows, z, dest, plan[3:4, :])])
    left = iota((1, 128), 1) < slots
    merged = []
    for f in range(5):
        halves = [
            jnp.where(left, columns[c][f], pltpu.roll(columns[c + 1][f], slots, 1)) for c in (0, 2)
        ]
        merged.append(jnp.concatenate(halves, 1))
    meets, rows, z, dest, kind = merged
    wide = 256
    upper = (iota((wide, wide), 0) <= iota((wide, wide), 1)).astype(jnp.bfloat16)
    row8 = iota((8, wide), 0)
    picked = jnp.where((meets == 1) & (kind == row8), 1.0, 0.0)
    order = mm(picked.astype(jnp.bfloat16), upper)
    place = iota((wide, wide), 0).astype(jnp.float32) + 1.0
    fields = jnp.where(row8 == 0, rows, jnp.where(row8 == 1, z, jnp.where(row8 == 2, dest, 0)))
    f_high, f_low = split(fields.astype(jnp.float32))
    across = (((1,), (1,)), ((), ()))
    for s in range(2):
        total = jnp.sum(picked[s : s + 1, :], axis=1, keepdims=True)
        spot = jnp.where(picked[s : s + 1, :] > 0.5, order[s : s + 1, :], 0.0)
        onehot = (spot == place).astype(jnp.bfloat16)
        got = lax.dot_general(f_high, onehot, across, preferred_element_type=jnp.float32)
        got = got + lax.dot_general(f_low, onehot, across, preferred_element_type=jnp.float32)
        got = jnp.where(row8 == 3, total, got)
        list_ref[s] = (got + 0.5).astype(jnp.int32)
    loads[2].wait()
    turn_shapes(shape_ref, turned, high_ref, low_ref, 1)

    loads[3].wait()
    for copy in second:
        copy.wait()
    fxp[0] = grecv_x[0]
    fxp[wx + 1] = grecv_x[1]
    fyp[:, 7, :] = grecv_y[0]
    fyp[:, wy + 8, :] = grecv_y[1]
    flux_ends = join_ends(grecv_z[0], grecv_z[1])

    def pot_step(x):
        here = fz[x]
        end = pltpu.roll(flux_ends, depth - 1 - 2 * x, 1)
        after = jnp.where(lane == depth - 1, end, pltpu.roll(here, depth - 1, 1))
        before = jnp.where(lane == 0, end, pltpu.roll(here, 1, 1))
        spread = (fxp[x + 2] - fxp[x]) * HALF
        spread = spread + (fyp[x, 9 : wy + 9, :] - fyp[x, 7 : wy + 7, :]) * HALF
        spread = spread + (after - before) * HALF
        pot_ref[x] = hart_ref[x] + slope_n_ref[x] - 2.0 * spread

    def pot_steps(t, carry):
        for k in range(per):
            pot_step(t * per + k)
        return carry

    lax.fori_loop(0, wx // per, pot_steps, 0)


def moment_kernel(
    depth_all, list_ref, pot_hbm, high_hbm, low_hbm, out_pot_ref, out_ref,
    pot_ref, high_ref, low_ref, padded, gathered, folded, sums, load_sems, sem,
):
    loads = [
        pltpu.make_async_copy(src, dst, load_sems.at[i])
        for i, (src, dst) in enumerate(
            ((pot_hbm, pot_ref), (high_hbm, high_ref), (low_hbm, low_ref))
        )
    ]
    for load in loads:
        load.start()
    wx, wy, depth = pot_ref.shape
    rows_y = wy + 2 * PAD
    comps = high_ref.shape[1] // BOX
    padded[...] = jnp.zeros_like(padded)
    sums[...] = jnp.zeros_like(sums)
    folded[...] = jnp.zeros_like(folded)
    loads[0].wait()
    store = pltpu.make_async_copy(pot_ref, out_pot_ref, sem)
    store.start()
    for x in range(wx):
        start = (x + PAD) * rows_y + PAD
        padded[start : start + wy, :] = pot_ref[x]
    loads[1].wait()
    loads[2].wait()
    lanes = GROUP * BOX
    per_tile = 128 // BOX
    lane = iota((BOX, 128), 1)
    adder = (iota((GROUP, lanes), 0) == iota((GROUP, lanes), 1) // BOX).astype(jnp.float32)
    keep = lax.rem(iota((BOX, lanes), 1), BOX) == iota((BOX, lanes), 0)

    for s in range(2):
        total = list_ref[s, 3, 0]

        def one_group(g, carry, s=s, total=total):
            for tile in range(lanes // 128):
                first = g * GROUP + tile * per_tile
                across = slice(tile * 128, (tile + 1) * 128)

                @pl.when(first < total)
                def _(first=first, across=across):
                    plan = []
                    for q in range(per_tile):
                        left = q * BOX
                        z = list_ref[s, 1, first + q]
                        shift = lax.rem(left + depth_all - z, depth)
                        cell = z + lane - left
                        cell = jnp.where(cell >= depth_all, cell - depth_all, cell)
                        mine = (lane >= left) & (lane < left + BOX) & (cell < depth)
                        plan.append((list_ref[s, 0, first + q], shift, mine))
                    for i in range(BOX):
                        made = jnp.zeros((BOX, 128), jnp.float32)
                        for row, shift, mine in plan:
                            piece = padded[pl.ds(row + i * rows_y, BOX), :]
                            made = jnp.where(mine, pltpu.roll(piece, shift, 1), made)
                        gathered[i * BOX : (i + 1) * BOX, across] = made

                @pl.when(first >= total)
                def _(across=across):
                    gathered[:, across] = jnp.zeros((BOX * BOX, 128), jnp.float32)

            g_high, g_low = split(gathered[...])
            product = mm(high_ref[s], g_high) + (mm(high_ref[s], g_low) + mm(low_ref[s], g_high))
            product = jnp.where(keep[None], product.reshape(comps, BOX, lanes), 0.0)
            folded[0:comps, :] = jnp.sum(product, axis=1)
            result = lax.dot_general(
                adder, folded[...], (((1,), (1,)), ((), ())), precision=PRECISE,
                preferred_element_type=jnp.float32,
            ) * (GRID_H**3)
            for q in range(GROUP):
                spot = list_ref[s, 2, g * GROUP + q]
                sums[pl.ds(spot, 1), :] = result[q : q + 1, :]
            return carry

        lax.fori_loop(0, (total + GROUP - 1) // GROUP, one_group, 0)
    slots = (sums.shape[0] - 8) // 4
    for c in range(4):
        held = jnp.zeros(out_ref.shape[1:], jnp.float32)
        for r in range(slots // GROUP):
            start = 8 + c * slots + r * GROUP
            held = held + pltpu.roll(sums[start : start + GROUP, :], r * LANES, 1)
        out_ref[c] = held
    store.wait()


def block_kernel(
    part_ref, species_ref, count_ref, coupling_ref, coulomb_hbm, rho_hbm, ham_ref,
    coulomb_ref, rho_ref, load_sems, around, parts, total_ref, cpad, send_sems, recv_sems,
):
    bands = lax.axis_size("band")
    me = lax.axis_index("band")
    slots = rho_ref.shape[0]
    up_x, down_x = {"dx": shifted("dx", 1)}, {"dx": shifted("dx", -1)}
    up_y, down_y = {"dyz": shifted("dyz", 1)}, {"dyz": shifted("dyz", -1)}
    up_xy = {"dx": shifted("dx", 1), "dyz": shifted("dyz", 1)}
    down_xy = {"dx": shifted("dx", -1), "dyz": shifted("dyz", -1)}
    others = [{"band": shifted("band", t)} for t in range(1, bands)]
    loads = [
        pltpu.make_async_copy(coulomb_hbm, coulomb_ref, load_sems.at[0]),
        pltpu.make_async_copy(rho_hbm, rho_ref, load_sems.at[1]),
    ]
    for load in loads:
        load.start()
    enter([up_x, down_x, up_y, down_y, up_xy, down_xy] + others)

    def remote(src, dst, sem, device):
        copy = pltpu.make_async_remote_copy(
            src_ref=src, dst_ref=dst, send_sem=send_sems.at[sem], recv_sem=recv_sems.at[sem],
            device_id=device, device_id_type=MESH,
        )
        copy.start()
        return copy

    copies = [
        remote(part_ref.at[c + 1], around.at[c], c, device)
        for c, device in enumerate((down_x, down_y, down_xy))
    ]
    eye = iota((slots, slots), 0) == iota((slots, slots), 1)
    kind = jnp.sum(jnp.where(eye, species_ref[...], 0), axis=1, keepdims=True)
    live = iota((slots, 1), 0) < count_ref[0]
    cpad[...] = jnp.zeros_like(cpad)
    comps = coupling_ref.shape[0]
    for load in loads:
        load.wait()
    rho_high, rho_low = split(rho_ref[...])
    coul = jnp.zeros(rho_ref.shape, jnp.float32)
    for s in range(2):
        cpad[s, 0:comps, :] = coupling_ref[:, s, :]
        c_high, c_low = split(coulomb_ref[s])
        term = mm(rho_high, c_high) + (mm(rho_high, c_low) + mm(rho_low, c_high))
        coul = jnp.where(kind == s, 2.0 * term, coul)
    for copy in copies:
        copy.wait()
    mine = (part_ref[0] + around[0]) + (around[1] + around[2])
    total_ref[...] = mine
    parts[me] = mine
    copies = [
        remote(total_ref, parts.at[me], 2 + t, others[t - 1]) for t in range(1, bands)
    ]
    for copy in copies:
        copy.wait()
    moments = (parts[0] + parts[1]) + (parts[2] + parts[3])
    for b in range(4, bands):
        moments = moments + parts[b]
    rows = [pltpu.roll(moments, (128 - r * LANES) % 128, 1) for r in range(slots // GROUP)]
    moments = jnp.concatenate(rows, 0)[:, 0:LANES]
    summed = jnp.zeros(rho_ref.shape, jnp.float32)
    for s in range(2):
        term = jnp.dot(moments, cpad[s], precision=PRECISE, preferred_element_type=jnp.float32)
        summed = jnp.where(kind == s, term, summed)
    ham_ref[...] = jnp.where(live, summed + coul, 0.0)


def apply_kernel(ham_ref, proj_hbm, out_ham_ref, out_hbm, proj_ref, out_ref, load_sems, sems):
    loads = []
    for t in range(ham_ref.shape[0] // NI):
        rows = pl.ds(t * NI * NI, NI * NI)
        loads.append(pltpu.make_async_copy(proj_hbm.at[rows], proj_ref.at[rows], load_sems.at[t]))
        loads[-1].start()
    out_ham_ref[...] = ham_ref[...]
    stores = []
    square = NI * NI
    row, col = iota((square, square), 0), iota((square, square), 1)
    spread = (lax.rem(row, NI) == lax.rem(col, NI)).astype(jnp.bfloat16)
    same_i = lax.rem(row, NI) == col // NI
    same_a = row // NI == col // NI
    for t in range(ham_ref.shape[0] // NI):
        block = ham_ref[t * NI : (t + 1) * NI, :]
        tall = jnp.broadcast_to(block[:, None, :], (NI, NI, square)).reshape(square, square)
        high, low = split(jnp.where(same_i, tall, 0.0))
        d_high = jnp.where(same_a, mm(high, spread), 0.0).astype(jnp.bfloat16)
        d_low = jnp.where(same_a, mm(low, spread), 0.0).astype(jnp.bfloat16)
        loads[t].wait()
        p_high, p_low = split(proj_ref[t * square : (t + 1) * square, :])
        out_ref[t * square : (t + 1) * square, :] = mm(d_high, p_high) + (
            mm(d_high, p_low) + mm(d_low, p_high)
        )
        rows = pl.ds(t * square, square)
        stores.append(pltpu.make_async_copy(out_ref.at[rows], out_hbm.at[rows], sems.at[t]))
        stores[-1].start()
    for store in stores:
        store.wait()


def local(
    density, hartree, box_root, species, atom_count, shape_functions, coupling, coulomb, rho_ij, projections
):
    f32 = jnp.float32
    wx, wy, depth = density.shape
    bands = lax.axis_size("band")
    slots = box_root.shape[1]
    kinds, comps, cells = shape_functions.shape
    vmem = pl.BlockSpec(memory_space=pltpu.VMEM)
    hbm = pl.BlockSpec(memory_space=pltpu.HBM)
    smem = pl.BlockSpec(memory_space=pltpu.SMEM)
    species_row = species.reshape(1, slots)

    face = lambda *s: pltpu.VMEM(s, f32)
    turned_shape = jax.ShapeDtypeStruct((kinds, comps * BOX, BOX * BOX), jnp.bfloat16)
    potential, atoms, high, low = pl.pallas_call(
        grid_kernel,
        name="grid_kernel",
        out_shape=(
            jax.ShapeDtypeStruct((wx, wy, depth), f32),
            jax.ShapeDtypeStruct((2, 8, 256), jnp.int32),
            turned_shape,
            turned_shape,
        ),
        in_specs=[hbm, hbm, hbm, vmem, vmem, smem],
        out_specs=(vmem,) * 4,
        scratch_shapes=[
            face(wx, wy, depth), face(wx, wy, depth), face(kinds, comps, cells),
            face(BOX * BOX, 128), pltpu.SemaphoreType.DMA((4,)),
            face(wx + 2, wy + 16, depth), face(wx + 2, wy, depth), face(wx, wy + 16, depth),
            face(wx, wy, depth), face(wx, wy, depth),
            face(2, wy, depth), face(2, wx, depth), face(wy, depth),
            face(2, wy, depth), face(2, wx, depth), face(2, wy, depth),
            face(2, wy, depth), face(2, wx, depth), face(wy, depth),
            face(2, wy, depth), face(2, wx, depth), face(2, wy, depth),
            pltpu.VMEM((8, 128), jnp.int32), pltpu.VMEM((3, 8, 128), jnp.int32),
            pltpu.SemaphoreType.DMA((15,)), pltpu.SemaphoreType.DMA((15,)),
        ],
        compiler_params=pltpu.CompilerParams(
            collective_id=0, has_side_effects=True, vmem_limit_bytes=56 * 1024 * 1024
        ),
    )(density, hartree, shape_functions.transpose(1, 0, 2), box_root, species_row, atom_count)

    lanes = GROUP * BOX
    potential, partial = pl.pallas_call(
        functools.partial(moment_kernel, depth * bands),
        name="moment_kernel",
        out_shape=(
            jax.ShapeDtypeStruct((wx, wy, depth), f32),
            jax.ShapeDtypeStruct((4, GROUP, 128), f32),
        ),
        in_specs=[smem, hbm, hbm, hbm],
        out_specs=(hbm, vmem),
        scratch_shapes=[
            face(wx, wy, depth),
            pltpu.VMEM(turned_shape.shape, jnp.bfloat16), pltpu.VMEM(turned_shape.shape, jnp.bfloat16),
            face((wx + 2 * PAD) * (wy + 2 * PAD), depth),
            face(BOX * BOX, lanes), face(128, lanes), face(8 + 4 * slots, 128),
            pltpu.SemaphoreType.DMA((3,)), pltpu.SemaphoreType.DMA,
        ],
        compiler_params=pltpu.CompilerParams(vmem_limit_bytes=VMEM_LIMIT),
    )(atoms, potential, high, low)

    ham = pl.pallas_call(
        block_kernel,
        name="block_kernel",
        out_shape=jax.ShapeDtypeStruct(rho_ij.shape, f32),
        in_specs=[vmem, vmem, smem, vmem, hbm, hbm],
        out_specs=vmem,
        scratch_shapes=[
            face(*coulomb.shape), face(*rho_ij.shape), pltpu.SemaphoreType.DMA((2,)),
            face(3, GROUP, 128), face(bands, GROUP, 128), face(GROUP, 128), face(2, LANES, NI * NI),
            pltpu.SemaphoreType.DMA((2 + bands,)), pltpu.SemaphoreType.DMA((2 + bands,)),
        ],
        compiler_params=pltpu.CompilerParams(
            collective_id=1, has_side_effects=True, vmem_limit_bytes=20 * 1024 * 1024
        ),
    )(partial, species_row, atom_count, coupling.transpose(1, 0, 2), coulomb, rho_ij)

    width = projections.shape[2]
    ham, applied = pl.pallas_call(
        apply_kernel,
        name="apply_kernel",
        out_shape=(
            jax.ShapeDtypeStruct(rho_ij.shape, f32),
            jax.ShapeDtypeStruct((slots * NI, width), f32),
        ),
        in_specs=[vmem, hbm],
        out_specs=(vmem, hbm),
        scratch_shapes=[
            face(slots * NI, width), face(slots * NI, width),
            pltpu.SemaphoreType.DMA((slots // NI,)), pltpu.SemaphoreType.DMA((slots // NI,)),
        ],
        compiler_params=pltpu.CompilerParams(vmem_limit_bytes=20 * 1024 * 1024),
    )(ham, projections.reshape(slots * NI, width))
    return potential, ham, applied.reshape(slots, NI, width)


def solution(mesh):
    in_specs = (
        P("dx", "dyz", "band"),
        P("dx", "dyz", "band"),
        P(None, ("dx", "dyz")),
        P(("dx", "dyz")),
        P(("dx", "dyz")),
        P(),
        P(),
        P(),
        P(("dx", "dyz"), None),
        P(("dx", "dyz"), None, "band"),
    )
    out_specs = (P("dx", "dyz", "band"), P(("dx", "dyz"), None), P(("dx", "dyz"), None, "band"))
    return jax.shard_map(local, mesh=mesh, in_specs=in_specs, out_specs=out_specs, check_vma=False)
```
